256 devices in a mesh: gx: 16 (over z, y_lo), gy: 4 (over y_hi, core), gz: 4 (over x).
Axes of the slice: x: 4, y: 4 (y_hi: 2, y_lo: 2; y = y_hi * 2 + y_lo), z: 8, core: 2. Of those that a mesh axis runs over, the one named last changes fastest.
Arguments:
- seg_rel: float32 [3, 1048576], P(None, ('gx', 'gy', 'gz')), may hold values from -0.5 to 0.5
- burgers: float32 [3, 1048576], P(None, ('gx', 'gy', 'gz')), may hold values from -5 to 5
- line_vec: float32 [3, 1048576], P(None, ('gx', 'gy', 'gz')), may hold values from -5 to 5
- seg_cell: int32 [1048576], P(('gx', 'gy', 'gz')), may hold values from 0 to 15
- ghost_tiles: int32 [2048], P(('gx', 'gy', 'gz')), may hold values from 0 to 31
- ghost_count: int32 [256], P(('gx', 'gy', 'gz')), may hold values from 1 to 8, as said below
- pair_target: int32 [32768], P(('gx', 'gy', 'gz')), may hold values from 0 to 31
- pair_source: int32 [32768], P(('gx', 'gy', 'gz')), may hold values from 0 to 247, as said below
- pair_group: int32 [32768], P(('gx', 'gy', 'gz')), may hold values from 0 to 1
- pair_count: int32 [256], P(('gx', 'gy', 'gz')), may hold values from 16 to 128, as said below
- node_dest: int32 [2, 1048576], P(None, ('gx', 'gy', 'gz')), may hold values from 0 to 107519, as said below
Outputs:
- new_offset: float32 [3, 1048576], P(None, ('gx', 'gy', 'gz'))
- node_force: float32 [3, 1048576], P(None, ('gx', 'gy', 'gz'))
The draws below stay inside these ranges and needn't reach their ends.
Inputs may be any that keep to these rules, and one draw needn't show every extreme that they name: Each domain's ghost list is live in its first ghost_count entries; some domain has all 8 live. `pair_count`: some domain has all 128 slots live. `pair_source`: values below 32 name own tiles; 32 + 8 t + g names ghost g of the neighbour in slot t, never t = 13. `node_dest`: A value is t * 4096 + n with direction slot t below 27; when t is not 13, n is below 1024.
All inputs are finite; a program needn't handle non-finite values.
Results may differ from the reference program's by a relative error of at most 0.0003.
Values sent between devices are 32-bit elements; how exact they have to be, the bound alone decides.
A program may use at most 128 MiB of HBM per device.

```python
import jax
import jax.numpy as jnp
from jax import lax

TILE_DEV = 32
TILE = 128
COMP = 6
TERMS = 35
CELL_Y = 4
CELL_Z = 4
SWEEPS = 2
CELL_DEV = 16
SEG_DEV = 4096
GHOST_DEV = 8
NPAIR_DEV = 128
BND = 1024
NDOM = 256
SEGS = 1048576
GHOSTS = 2048
PAIRS = 32768
N_GX = 16
N_GY = 4
N_GZ = 4


def draw_ghost_count(key, part):
    key = jax.random.fold_in(key, 1)
    key_counts, key_top = jax.random.split(key)
    counts = jax.random.randint(key_counts, (NDOM,), 1, GHOST_DEV + 1)
    top_domain = jax.random.randint(key_top, (), 0, NDOM)
    return counts.at[top_domain].set(GHOST_DEV).astype(jnp.int32)


def draw_pair_source(key, part):
    key = jax.random.fold_in(key, 2)
    key_pick, key_own, key_slot, key_ghost, key_ends = jax.random.split(key, 5)
    total = NPAIR_DEV * NDOM
    extent = (total,)
    picked = jax.random.randint(key_pick, extent, 0, 2)
    own_ids = jax.random.randint(key_own, extent, 0, TILE_DEV)
    slot_ids = jax.random.randint(key_slot, extent, 0, 26)
    slot_ids = slot_ids + (slot_ids >= 13).astype(jnp.int32)
    ghost_ids = TILE_DEV + slot_ids * GHOST_DEV + jax.random.randint(key_ghost, extent, 0, GHOST_DEV)
    values = jnp.where(picked == 0, own_ids, ghost_ids)
    low_at = jax.random.randint(key_ends, (), 0, total)
    high_at = (low_at + 1) % total
    values = values.at[low_at].set(0).at[high_at].set(TILE_DEV + 27 * GHOST_DEV - 1)
    return values.astype(jnp.int32)


def draw_pair_count(key, part):
    key = jax.random.fold_in(key, 3)
    key_counts, key_top = jax.random.split(key)
    spread = jax.random.randint(key_counts, (NDOM,), 0, 7 * NPAIR_DEV // 8 + 1)
    counts = NPAIR_DEV // 8 + spread * spread // NPAIR_DEV
    top_domain = jax.random.randint(key_top, (), 0, NDOM)
    return counts.at[top_domain].set(NPAIR_DEV).astype(jnp.int32)


def draw_node_dest(key, part):
    key = jax.random.fold_in(key, 4)
    key_far, key_dir, key_own, key_edge, key_ends = jax.random.split(key, 5)
    total = SEG_DEV * NDOM
    extent = (2, total)
    remote = jax.random.randint(key_far, extent, 0, 4) == 0
    direction = jnp.where(remote, jax.random.randint(key_dir, extent, 0, 27), 13)
    slot_ids = jnp.where(direction == 13, jax.random.randint(key_own, extent, 0, SEG_DEV), jax.random.randint(key_edge, extent, 0, BND))
    values = (direction * SEG_DEV + slot_ids).reshape(-1)
    low_at = jax.random.randint(key_ends, (), 0, 2 * total)
    high_at = (low_at + 1) % (2 * total)
    values = values.at[low_at].set(0).at[high_at].set(26 * SEG_DEV + BND - 1)
    return values.reshape(2, total).astype(jnp.int32)


def place_ends(array, key, least, largest):
    shape = array.shape
    place = [jax.random.randint(jax.random.fold_in(key, axis), (), 0, shape[axis]) for axis in range(len(shape))]
    array = array.at[tuple(place)].set(least)
    longest = shape.index(max(shape))
    place[longest] = (place[longest] + 1) % shape[longest]
    return array.at[tuple(place)].set(largest)


def level_of(own_key, shape, shards, least, high):
    loudness = 1.0
    for axis_at, blocks in shards:
        heights = jax.random.uniform(jax.random.fold_in(jax.random.fold_in(own_key, 6), axis_at), (blocks,), jnp.float32, least / len(shards), high / len(shards))
        loudness = loudness * jnp.repeat(jnp.exp(heights), shape[axis_at] // blocks).reshape((-1,) + (1,) * (len(shape) - 1 - axis_at))
    return loudness


def normal_values(key, shape, scale, limit, cuts=(), held_as=jnp.bfloat16):
    array = jax.random.normal(key, shape, jnp.float32) * scale
    if len(cuts) > 0:
        array = level_of(key, shape, cuts, -0.22, 0.18) * array
    return jnp.clip(array, min=-limit, max=limit).astype(held_as)


def setup_inputs(seed: int = 0) -> dict:
    splits = jax.random.split(jax.random.key(seed), 12)
    return {
        "seg_rel": jnp.clip(jax.random.uniform(splits[0], (3, SEGS), jnp.float32, -0.5, 0.5) * level_of(splits[0], (3, SEGS), ((1, 256),), -0.4, 0.0), -0.5, 0.5),
        "burgers": normal_values(splits[1], (3, SEGS), 1.0, 5.0, ((1, 256),), jnp.float32),
        "line_vec": normal_values(splits[2], (3, SEGS), 1.0, 5.0, ((1, 256),), jnp.float32),
        "seg_cell": place_ends(jax.random.randint(splits[3], (SEGS,), 0, CELL_DEV), jax.random.fold_in(splits[3], 1), 0, CELL_DEV - 1).astype(jnp.int32),
        "ghost_tiles": place_ends(jax.random.randint(splits[4], (GHOSTS,), 0, TILE_DEV), jax.random.fold_in(splits[4], 1), 0, TILE_DEV - 1).astype(jnp.int32),
        "ghost_count": draw_ghost_count(jax.random.fold_in(splits[11], 71), 0),
        "pair_target": place_ends(jax.random.randint(splits[6], (PAIRS,), 0, TILE_DEV), jax.random.fold_in(splits[6], 1), 0, TILE_DEV - 1).astype(jnp.int32),
        "pair_source": draw_pair_source(jax.random.fold_in(splits[11], 71), 0),
        "pair_group": place_ends(jax.random.randint(splits[8], (PAIRS,), 0, 2), jax.random.fold_in(splits[8], 1), 0, 1).astype(jnp.int32),
        "pair_count": draw_pair_count(jax.random.fold_in(splits[11], 71), 0),
        "node_dest": draw_node_dest(jax.random.fold_in(splits[11], 71), 0),
    }


CORE2 = 0.25
NEAR_SCALE = 0.05
FAR_SCALE = 0.002
STEP_SIZE = 0.1
HIGH = lax.Precision.HIGHEST
exponents = [(a, b, degree - a - b) for degree in range(5) for a in range(degree, -1, -1) for b in range(degree - a, -1, -1)]

def monomials(unit):
    return jnp.stack([unit[0] ** a * unit[1] ** b * unit[2] ** c for a, b, c in exponents])

def symmetric_part(burgers, line_vec):
    return jnp.stack([burgers[0] * line_vec[0], burgers[1] * line_vec[1], burgers[2] * line_vec[2], 0.5 * (burgers[0] * line_vec[1] + burgers[1] * line_vec[0]), 0.5 * (burgers[1] * line_vec[2] + burgers[2] * line_vec[1]), 0.5 * (burgers[0] * line_vec[2] + burgers[2] * line_vec[0])])

def moment_terms(offset, burgers, line_vec):
    table = symmetric_part(burgers, line_vec)[:, None, :] * monomials(2.0 * offset)[None, :, :]
    return table.reshape(COMP * TERMS, offset.shape[-1])

def stress_force(per_segment, offset, burgers, line_vec):
    stress = lax.optimization_barrier(jnp.sum(per_segment.reshape(COMP, TERMS, -1) * monomials(2.0 * offset)[None], axis=1))
    push_x = stress[0] * burgers[0] + stress[3] * burgers[1] + stress[5] * burgers[2]
    push_y = stress[3] * burgers[0] + stress[1] * burgers[1] + stress[4] * burgers[2]
    push_z = stress[5] * burgers[0] + stress[4] * burgers[1] + stress[2] * burgers[2]
    return jnp.stack([push_y * line_vec[2] - push_z * line_vec[1], push_z * line_vec[0] - push_x * line_vec[2], push_x * line_vec[1] - push_y * line_vec[0]])

def pair_force(targets, sources):
    separation = targets[0:3, :, :, None] - sources[0:3, :, None, :]
    radius2 = lax.optimization_barrier(jnp.sum(separation * separation, axis=0)) + CORE2
    inverse3 = 1.0 / (radius2 * jnp.sqrt(radius2))
    burg_dot = lax.optimization_barrier(jnp.sum(targets[3:6, :, :, None] * sources[3:6, :, None, :], axis=0))
    line_dot = lax.optimization_barrier(jnp.sum(targets[6:9, :, :, None] * sources[6:9, :, None, :], axis=0))
    weight = burg_dot * line_dot * inverse3
    return lax.optimization_barrier(jnp.sum(weight[None] * separation, axis=-1))

def cell_coords(along_x, along_y, along_z, local):
    return jnp.stack([along_x + 0 * local, along_y * CELL_Y + local // CELL_Z, along_z * CELL_Z + local % CELL_Z]).astype(jnp.float32)

def place_of(device):
    return (device // (N_GY * N_GZ), device // N_GZ % N_GY, device % N_GZ)

def near_forces(buffer, target_ids, source_ids, weights):
    block_pairs = 16
    tile_ids = jnp.arange(TILE_DEV, dtype=jnp.int32)

    def advance(running, block_ids):
        target_block, source_block, weight_block = block_ids
        contrib = pair_force(buffer[:, target_block], buffer[:, source_block])
        select = (target_block[:, None] == tile_ids[None, :]).astype(jnp.float32) * weight_block[:, None]
        return (running + jnp.einsum('pn,cpi->cni', select, contrib, precision=HIGH), None)
    blocks = (target_ids.reshape(-1, block_pairs), source_ids.reshape(-1, block_pairs), weights.reshape(-1, block_pairs))
    result, unused = lax.scan(advance, jnp.zeros((3, TILE_DEV, TILE), jnp.float32), blocks)
    return result.reshape(3, TILE_DEV * TILE)

def reference(seg_rel, burgers, line_vec, seg_cell, ghost_tiles, ghost_count, pair_target, pair_source, pair_group, pair_count, node_dest):
    domains = N_GX * N_GY * N_GZ
    device_ids = jnp.arange(domains, dtype=jnp.int32)
    offsets = seg_rel.reshape(3, domains, SEG_DEV).transpose(1, 0, 2)
    burg_all = burgers.reshape(3, domains, SEG_DEV).transpose(1, 0, 2)
    line_all = line_vec.reshape(3, domains, SEG_DEV).transpose(1, 0, 2)
    cells = seg_cell.reshape(domains, SEG_DEV)
    place_x, place_y, place_z = place_of(device_ids[:, None])
    anchors = jnp.moveaxis(cell_coords(place_x, place_y, place_z, cells), 0, 1)
    local_ids = jnp.arange(CELL_DEV, dtype=jnp.int32)

    def moments(inputs):
        offset, burg, line, cell = inputs
        onehot = (local_ids[:, None] == cell[None, :]).astype(jnp.float32)
        return jnp.dot(moment_terms(offset, burg, line), onehot.T, precision=HIGH)
    moment_all = lax.map(moments, (offsets, burg_all, line_all, cells))
    moment_grid = moment_all.transpose(1, 0, 2).reshape(COMP * TERMS, domains * CELL_DEV)
    all_cells = jnp.arange(domains * CELL_DEV, dtype=jnp.int32)
    cell_x, cell_y, cell_z = place_of(all_cells // CELL_DEV)
    coords = cell_coords(cell_x, cell_y, cell_z, all_cells % CELL_DEV)
    distance2 = jnp.zeros((domains * CELL_DEV, domains * CELL_DEV), jnp.float32)
    for axis_id in range(3):
        spacing = coords[axis_id][:, None] - coords[axis_id][None, :]
        distance2 = distance2 + spacing * spacing
    kernel = jnp.where(distance2 > 3.5, 1.0 / jnp.sqrt(jnp.maximum(distance2, 1.0)), 0.0)
    expansion = jnp.dot(moment_grid, kernel, precision=HIGH)
    expansion = expansion.reshape(COMP * TERMS, domains, CELL_DEV).transpose(1, 0, 2)
    ghost_list = ghost_tiles.reshape(domains, GHOST_DEV)
    target_all = pair_target.reshape(domains, NPAIR_DEV)
    source_all = pair_source.reshape(domains, NPAIR_DEV)
    group_all = pair_group.reshape(domains, NPAIR_DEV)
    live_ghost = (jnp.arange(GHOST_DEV, dtype=jnp.int32)[None, :] < ghost_count[:, None]).astype(jnp.float32)
    live_pairs = jnp.arange(NPAIR_DEV, dtype=jnp.int32)[None, :] < pair_count[:, None]
    dest = node_dest.reshape(2, domains, SEG_DEV)
    direction = dest // SEG_DEV
    slot_ids = dest % SEG_DEV
    owner_x = place_x[None] + direction // 9 - 1
    owner_y = place_y[None] + direction // 3 % 3 - 1
    owner_z = place_z[None] + direction % 3 - 1
    owner_in = (owner_x >= 0) & (owner_x < N_GX) & (owner_y >= 0) & (owner_y < N_GY) & (owner_z >= 0) & (owner_z < N_GZ)
    owner = (owner_x * N_GY + owner_y) * N_GZ + owner_z
    node_ids = jnp.where(owner_in, owner * SEG_DEV + slot_ids, domains * SEG_DEV).reshape(-1)
    node_total = jnp.zeros((3, domains * SEG_DEV), jnp.float32)

    def pick_ghosts(own_tiles, chosen):
        return own_tiles[:, chosen]
    for sweep in range(SWEEPS):
        positions = anchors + 0.5 + offsets
        tiles = jnp.concatenate([positions, burg_all, line_all], axis=1).reshape(domains, 9, TILE_DEV, TILE)
        payload = jax.vmap(pick_ghosts)(tiles, ghost_list) * live_ghost[:, None, :, None]
        active_all = (live_pairs & (group_all == sweep)).astype(jnp.float32)

        def near_domain(inputs):
            device, own_tiles, target_ids, source_ids, weights = inputs
            home_x, home_y, home_z = place_of(device)
            pieces = [own_tiles]
            for step_x in (-1, 0, 1):
                for step_y in (-1, 0, 1):
                    for step_z in (-1, 0, 1):
                        next_x = home_x + step_x
                        next_y = home_y + step_y
                        next_z = home_z + step_z
                        inside = (next_x >= 0) & (next_x < N_GX) & (next_y >= 0) & (next_y < N_GY) & (next_z >= 0) & (next_z < N_GZ)
                        neighbour = (jnp.clip(next_x, 0, N_GX - 1) * N_GY + jnp.clip(next_y, 0, N_GY - 1)) * N_GZ + jnp.clip(next_z, 0, N_GZ - 1)
                        pieces.append(payload[neighbour] * inside.astype(jnp.float32))
            buffer = jnp.concatenate(pieces, axis=1)
            return near_forces(buffer, target_ids, source_ids, weights)
        near_all = lax.map(near_domain, (device_ids, tiles, target_all, source_all, active_all))

        def far_domain(inputs):
            local_exp, offset, burg, line, cell = inputs
            onehot = (local_ids[:, None] == cell[None, :]).astype(jnp.float32)
            per_segment = jnp.dot(local_exp, onehot, precision=HIGH)
            return stress_force(per_segment, offset, burg, line)
        far_all = lax.map(far_domain, (expansion, offsets, burg_all, line_all, cells))
        forces = FAR_SCALE * far_all + NEAR_SCALE * near_all
        offsets = offsets + STEP_SIZE * forces
        halves = 0.5 * forces.transpose(1, 0, 2)
        values = jnp.broadcast_to(halves[:, None], (3, 2, domains, SEG_DEV)).reshape(3, -1)
        added = jax.ops.segment_sum(values.T, node_ids, domains * SEG_DEV + 1)[:domains * SEG_DEV]
        node_total = node_total + added.T
    return (offsets.transpose(1, 0, 2).reshape(3, domains * SEG_DEV), node_total)
```

```python
import functools

import jax
import jax.numpy as jnp
from jax import lax
from jax.experimental import pallas as pl
from jax.experimental.pallas import tpu as pltpu
from jax.sharding import PartitionSpec as P

TILE = 128
SEG = 4096
GROUPS = 4
GHOST_DEV = 8
CELL_DEV = 16
COMP = 6
TERMS = 35
LANE_STEP = 42
PAIRS = 128
CORE2 = 0.25
NEAR_SCALE = 0.05
FAR_SCALE = 0.002
STEP_SIZE = 0.1
MESH = pl.DeviceIdType.MESH
F32 = jnp.float32
BF16 = jnp.bfloat16
EXPONENTS = [
    (a, b, degree - a - b)
    for degree in range(5)
    for a in range(degree, -1, -1)
    for b in range(degree - a, -1, -1)
]
NT = (((1,), (1,)), ((), ()))
TN = (((0,), (0,)), ((), ()))


def vmem(count):
    return [pl.BlockSpec(memory_space=pltpu.VMEM)] * count


def smem(count):
    return [pl.BlockSpec(memory_space=pltpu.SMEM)] * count


def halves_of(value):
    high = value.astype(BF16).astype(F32)
    return high, value - high


def powers(unit):
    square = unit * unit
    return [None, unit, square, square * unit, square * square]


def monomial(u, v, w, exps):
    result = None
    for table, power in zip((u, v, w), exps):
        if power:
            result = table[power] if result is None else result * table[power]
    return result


def symmetric(b, t):
    return [
        b[0] * t[0],
        b[1] * t[1],
        b[2] * t[2],
        0.5 * (b[0] * t[1] + b[1] * t[0]),
        0.5 * (b[1] * t[2] + b[2] * t[1]),
        0.5 * (b[0] * t[2] + b[2] * t[0]),
    ]


class Place:
    def __init__(self, sizes):
        self.sizes = sizes
        self.at = tuple(lax.axis_index(name) for name in ("gx", "gy", "gz"))

    def beside(self, slot, sign=1):
        steps = (slot // 9 - 1, slot // 3 % 3 - 1, slot % 3 - 1)
        where = tuple(a + sign * s for a, s in zip(self.at, steps))
        inside = slot != 13
        for at, size in zip(where, self.sizes):
            inside = jnp.logical_and(inside, jnp.logical_and(at >= 0, at < size))
        return where, inside

    def count_beside(self):
        total = 1
        for at, size in zip(self.at, self.sizes):
            total = total * (3 - (at == 0).astype(jnp.int32) - (at == size - 1).astype(jnp.int32))
        return total - 1


def each_slot(body):
    def step(slot, carry):
        body(slot)
        return carry

    lax.fori_loop(0, 27, step, 0)


def greet_neighbours(place, barrier):
    def greet(slot):
        where, inside = place.beside(slot)

        @pl.when(inside)
        def _():
            pl.semaphore_signal(barrier, inc=1, device_id=where, device_id_type=MESH)

    each_slot(greet)


def expand_kernel(
    sizes,
    rel_ref,
    burg_ref,
    line_ref,
    cell_ref,
    ghost_ref,
    live_ref,
    source_ref,
    base_ref,
    table_ref,
    own,
    payload,
    mono,
    symm,
    gathered,
    contrib,
    arrived,
    ghost_send,
    ghost_recv,
    plane_send,
    plane_recv,
    line_send,
    line_recv,
):
    nx, ny, nz = sizes
    plane = ny * nz
    place = Place(sizes)
    gx, gy, gz = place.at
    here = gy * nz + gz

    def plane_peer(step):
        peer = lax.rem(here + step, plane)
        return (gx, peer // nz, lax.rem(peer, nz))

    def line_peer(step):
        return (lax.rem(gx + step, nx), gy, gz)

    barrier = pltpu.get_barrier_semaphore()
    greet_neighbours(place, barrier)

    def greet_plane(step, carry):
        pl.semaphore_signal(barrier, inc=1, device_id=plane_peer(step), device_id_type=MESH)
        return carry

    def greet_line(step, carry):
        pl.semaphore_signal(barrier, inc=1, device_id=line_peer(step), device_id_type=MESH)
        return carry

    lax.fori_loop(1, plane, greet_plane, 0)
    lax.fori_loop(1, nx, greet_line, 0)

    for tile in range(SEG // TILE):
        lanes = pl.ds(tile * TILE, TILE)
        for row in range(3):
            own[tile // 8, row, pl.ds(tile % 8, 1), :] = rel_ref[pl.ds(row, 1), lanes]
            own[tile // 8, 3 + row, pl.ds(tile % 8, 1), :] = burg_ref[pl.ds(row, 1), lanes]
            own[tile // 8, 6 + row, pl.ds(tile % 8, 1), :] = line_ref[pl.ds(row, 1), lanes]
    for group in range(GROUPS):
        rows = slice(8 * group, 8 * group + 8)
        cell = cell_ref[rows, :]
        rel = [own[group, row] for row in range(3)]
        burg = [own[group, 3 + row] for row in range(3)]
        line = [own[group, 6 + row] for row in range(3)]
        corner = (
            jnp.full((8, TILE), gx, jnp.int32),
            gy * 4 + (cell >> 2),
            gz * 4 + (cell & 3),
        )
        for row in range(3):
            base = corner[row].astype(F32) + 0.5
            base_ref[group, row] = base
            own[group, row] = base + rel[row]
        source_ref[group] = own[group]
        for at, value in enumerate(symmetric(burg, line)):
            symm[pl.ds(at * 32 + 8 * group, 8), :] = value
        u, v, w = (powers(2.0 * value) for value in rel)
        for at, exps in enumerate(EXPONENTS):
            value = monomial(u, v, w, exps)
            mono[pl.ds(at * 32 + 8 * group, 8), :] = (
                jnp.ones((8, TILE), F32) if value is None else value
            )
    for at in range(TERMS, 40):
        mono[pl.ds(at * 32, 32), :] = jnp.zeros((32, TILE), F32)
    for ghost in range(GHOST_DEV):
        tile = ghost_ref[ghost]
        live = jnp.where(ghost < live_ref[0], 1.0, 0.0)
        for row in range(9):
            value = own[tile // 8, row, pl.ds(lax.rem(tile, 8), 1), :]
            payload[row, pl.ds(ghost, 1), :] = value * live

    cells = lax.broadcasted_iota(jnp.int32, (CELL_DEV, TILE), 0)
    moments = jnp.zeros((COMP * CELL_DEV, 40), F32)
    for block in range(4):
        lefts, rights = [], []
        for tile in range(8 * block, 8 * block + 8):
            chosen = cells == cell_ref[pl.ds(tile, 1), :]
            left = jnp.concatenate(
                [
                    jnp.where(chosen, symm[pl.ds(at * 32 + tile, 1), :], 0.0)
                    for at in range(COMP)
                ],
                axis=0,
            )
            right = mono[pl.ds(tile, 40, stride=32), :]
            left_high, left_low = halves_of(left)
            right_high, right_low = halves_of(right)
            lefts += [left_high, left_high, left_low]
            rights += [right_high, right_low, right_high]
        moments = moments + lax.dot_general(
            jnp.concatenate(lefts, axis=1).astype(BF16),
            jnp.concatenate(rights, axis=1).astype(BF16),
            NT,
            preferred_element_type=F32,
        )
    wide = jnp.concatenate([moments, jnp.zeros((COMP * CELL_DEV, TILE - 40), F32)], axis=1)
    mine = pl.ds(pl.multiple_of(here * CELL_DEV, CELL_DEV), CELL_DEV)
    for half in range(2):
        total = jnp.zeros((CELL_DEV, TILE), F32)
        for third in range(3):
            at = (3 * half + third) * CELL_DEV
            part = wide[at : at + CELL_DEV]
            total = total + (pltpu.roll(part, third * LANE_STEP, 1) if third else part)
        gathered[mine, pl.ds(half * TILE, TILE)] = total

    pl.semaphore_wait(barrier, place.count_beside() + plane - 1 + nx - 1)

    def plane_copy(step):
        return pltpu.make_async_remote_copy(
            src_ref=gathered.at[mine],
            dst_ref=gathered.at[mine],
            send_sem=plane_send.at[step],
            recv_sem=plane_recv.at[step],
            device_id=plane_peer(step),
            device_id_type=MESH,
        )

    def ghost_copy(slot):
        where, inside = place.beside(slot)
        copy = pltpu.make_async_remote_copy(
            src_ref=payload,
            dst_ref=source_ref.at[GROUPS + 26 - slot],
            send_sem=ghost_send.at[slot],
            recv_sem=ghost_recv.at[26 - slot],
            device_id=where,
            device_id_type=MESH,
        )
        return copy, inside

    def start_plane(step, carry):
        plane_copy(step).start()
        return carry

    lax.fori_loop(1, plane, start_plane, 0)

    def start_ghost(slot):
        copy, inside = ghost_copy(slot)

        @pl.when(inside)
        def _():
            copy.start()

        @pl.when(jnp.logical_not(inside))
        def _():
            source_ref[GROUPS + slot] = jnp.zeros((9, GHOST_DEV, TILE), F32)

    each_slot(start_ghost)

    rows, columns = nx * CELL_DEV, plane * CELL_DEV
    row = lax.broadcasted_iota(jnp.int32, (rows, columns), 0)
    column = lax.broadcasted_iota(jnp.int32, (rows, columns), 1)
    peer = column >> 4
    step_x = (row >> 4) - gx
    step_y = gy * 4 + ((row >> 2) & 3) - (peer // nz * 4 + ((column >> 2) & 3))
    step_z = gz * 4 + (row & 3) - (peer % nz * 4 + (column & 3))
    distance2 = (step_x * step_x + step_y * step_y + step_z * step_z).astype(F32)
    weight = jnp.where(distance2 > 3.5, 1.0 / jnp.sqrt(jnp.maximum(distance2, 1.0)), 0.0)

    def wait_plane(step, carry):
        plane_copy(step).wait()
        return carry

    lax.fori_loop(1, plane, wait_plane, 0)
    contrib[...] = jnp.dot(
        weight, gathered[...], precision=lax.Precision.HIGHEST, preferred_element_type=F32
    )

    def line_copy(step):
        there = lax.rem(gx + step, nx)
        return pltpu.make_async_remote_copy(
            src_ref=contrib.at[pl.ds(pl.multiple_of(there * CELL_DEV, CELL_DEV), CELL_DEV)],
            dst_ref=arrived.at[step],
            send_sem=line_send.at[step],
            recv_sem=line_recv.at[step],
            device_id=line_peer(step),
            device_id_type=MESH,
        )

    def start_line(step, carry):
        line_copy(step).start()
        return carry

    lax.fori_loop(1, nx, start_line, 0)
    total = contrib[pl.ds(pl.multiple_of(gx * CELL_DEV, CELL_DEV), CELL_DEV), :]

    def wait_line(step, carry):
        line_copy(step).wait()
        return carry

    lax.fori_loop(1, nx, wait_line, 0)
    for step in range(1, nx):
        total = total + arrived[step]
    full = jnp.concatenate([total, jnp.zeros((TILE - CELL_DEV, 2 * TILE), F32)], axis=0)
    table_ref[pl.ds(0, TILE), :] = full[:, :TILE].T
    table_ref[pl.ds(TILE, TILE), :] = full[:, TILE:].T
    source_ref[GROUPS + 13] = jnp.zeros((9, GHOST_DEV, TILE), F32)

    def wait_ghost_send(slot):
        copy, inside = ghost_copy(slot)

        @pl.when(inside)
        def _():
            copy.wait_send()

    def wait_ghost_recv(slot):
        copy, _ = ghost_copy(slot)
        _, inside = place.beside(slot, -1)

        @pl.when(inside)
        def _():
            copy.wait_recv()

    each_slot(wait_ghost_send)
    each_slot(wait_ghost_recv)


def far_force(group, offset, burg, line, cell, table_ref):
    u, v, w = (powers(2.0 * value) for value in offset)
    stress = [None] * COMP
    for at, exps in enumerate(EXPONENTS):
        value = monomial(u, v, w, exps)
        for comp in range(COMP):
            row = comp // 3 * TILE + comp % 3 * LANE_STEP + at
            entry = jnp.broadcast_to(table_ref[pl.ds(row, 1), :], (8, TILE))
            term = jnp.take_along_axis(entry, cell, axis=1, mode="promise_in_bounds")
            if value is not None:
                term = term * value
            stress[comp] = term if stress[comp] is None else stress[comp] + term
    push_x = stress[0] * burg[0] + stress[3] * burg[1] + stress[5] * burg[2]
    push_y = stress[3] * burg[0] + stress[1] * burg[1] + stress[4] * burg[2]
    push_z = stress[5] * burg[0] + stress[4] * burg[1] + stress[2] * burg[2]
    return [
        push_y * line[2] - push_z * line[1],
        push_z * line[0] - push_x * line[2],
        push_x * line[1] - push_y * line[0],
    ]


def split_rows(source_ref, group):
    highs, lows = [], []
    for a in range(3):
        for c in range(3):
            high, low = halves_of(source_ref[group, 3 + a] * source_ref[group, 6 + c])
            highs.append(high)
            lows.append(low)
    return highs, lows


def near_pass(
    sweep, count_ref, target_ref, from_ref, group_ref, source_ref, places, sides, targets, near, chosen
):
    zero = jnp.zeros((8, TILE), F32)

    def fill(group, carry):
        highs, lows = split_rows(source_ref, group)
        at = pl.multiple_of(group * 256, 256)
        for row, value in enumerate(highs + highs + lows + [zero] * 5):
            sides[pl.ds(at + 8 * row, 8), :] = value
        return carry

    lax.fori_loop(0, GROUPS + 27, fill, 0)
    for group in range(GROUPS):
        highs, lows = split_rows(source_ref, group)
        for row, value in enumerate(highs + lows + highs + [zero] * 5):
            targets[pl.ds(group * 256 + 8 * row, 8), :] = value
    near[...] = jnp.zeros(near.shape, F32)

    def choose(pair, used):
        chosen[used] = pair
        return used + (group_ref[pair] == sweep).astype(jnp.int32)

    used = lax.fori_loop(0, count_ref[0], choose, 0)

    def one(at, carry):
        pair = chosen[at]
        source = from_ref[pair]
        target = target_ref[pair]
        left = sides[pl.ds((source >> 3) * 256 + (source & 7), 32, stride=8), :]
        right = targets[pl.ds((target >> 3) * 256 + (target & 7), 32, stride=8), :]
        strength = lax.dot_general(
            left.astype(BF16), right.astype(BF16), TN, preferred_element_type=F32
        )
        there = places[pl.ds((source >> 3) * 64 + (source & 7), 8, stride=8), :].T
        spot = (target >> 3) * 64 + (target & 7)
        here = [places[pl.ds(spot + 8 * row, 1), :] for row in range(3)]
        totals = [jnp.zeros((8, TILE), F32)] * 3
        for chunk in range(16):
            span = slice(8 * chunk, 8 * chunk + 8)
            gaps = [here[row] - there[span, row : row + 1] for row in range(3)]
            radius2 = gaps[0] * gaps[0] + gaps[1] * gaps[1] + gaps[2] * gaps[2] + CORE2
            inverse = lax.rsqrt(radius2)
            weight = strength[span, :] * (inverse * inverse * inverse)
            totals = [total + weight * gap for total, gap in zip(totals, gaps)]
        spot = (target >> 3) * 24 + (target & 7)
        for row in range(3):
            at_row = pl.ds(spot + 8 * row, 1)
            near[at_row, :] += jnp.sum(totals[row], axis=0, keepdims=True)
        return carry

    lax.fori_loop(0, used, one, 0)


def forces_of(group, offsets, cell_ref, source_ref, table_ref, near):
    burg = [source_ref[group, 3 + row] for row in range(3)]
    line = [source_ref[group, 6 + row] for row in range(3)]
    cell = cell_ref[pl.ds(8 * group, 8), :]
    far = far_force(group, offsets, burg, line, cell, table_ref)
    return [
        FAR_SCALE * far[row] + NEAR_SCALE * near[pl.ds(group * 24 + 8 * row, 8), :]
        for row in range(3)
    ]


def first_kernel(
    count_ref,
    target_ref,
    from_ref,
    group_ref,
    ghost_ref,
    source_ref,
    base_ref,
    table_ref,
    cell_ref,
    rel_ref,
    offset_ref,
    force_ref,
    places_ref,
    payload_ref,
    places,
    sides,
    targets,
    near,
    chosen,
):
    def spread(group, carry):
        at = pl.multiple_of(group * 64, 64)
        for row in range(3):
            places[pl.ds(at + 8 * row, 8), :] = source_ref[group, row]
        return carry

    lax.fori_loop(0, GROUPS + 27, spread, 0)
    near_pass(
        0, count_ref, target_ref, from_ref, group_ref, source_ref, places, sides, targets, near, chosen
    )
    for tile in range(SEG // TILE):
        for row in range(3):
            offset_ref[tile // 8, row, pl.ds(tile % 8, 1), :] = rel_ref[
                pl.ds(row, 1), pl.ds(tile * TILE, TILE)
            ]
    for group in range(GROUPS):
        offsets = [offset_ref[group, row] for row in range(3)]
        forces = forces_of(group, offsets, cell_ref, source_ref, table_ref, near)
        for row in range(3):
            moved = offsets[row] + STEP_SIZE * forces[row]
            force_ref[group, row] = forces[row]
            offset_ref[group, row] = moved
            places_ref[group, row] = base_ref[group, row] + moved
    for ghost in range(GHOST_DEV):
        tile = ghost_ref[ghost]
        for row in range(3):
            payload_ref[row, pl.ds(ghost, 1), :] = places_ref[tile >> 3, row, pl.ds(tile & 7, 1), :]


def exchange(place, send_of, receive_at, send_sem, recv_sem):
    def copy_of(slot):
        where, inside = place.beside(slot)
        copy = pltpu.make_async_remote_copy(
            src_ref=send_of(slot),
            dst_ref=receive_at(26 - slot),
            send_sem=send_sem.at[slot],
            recv_sem=recv_sem.at[26 - slot],
            device_id=where,
            device_id_type=MESH,
        )
        return copy, inside

    def start(slot):
        copy, inside = copy_of(slot)

        @pl.when(inside)
        def _():
            copy.start()

    def wait(slot):
        copy, inside = copy_of(slot)

        @pl.when(inside)
        def _():
            copy.wait_send()

        arriving, _ = copy_of(26 - slot)

        @pl.when(inside)
        def _():
            arriving.wait_recv()

    return start, wait


def ghosts_kernel(sizes, payload_ref, ghosts_ref, send_sem, recv_sem):
    place = Place(sizes)
    barrier = pltpu.get_barrier_semaphore()
    greet_neighbours(place, barrier)

    def clear(slot):
        _, inside = place.beside(slot)

        @pl.when(jnp.logical_not(inside))
        def _():
            ghosts_ref[slot] = jnp.zeros((3, GHOST_DEV, TILE), F32)

    each_slot(clear)
    pl.semaphore_wait(barrier, place.count_beside())
    start, wait = exchange(
        place, lambda slot: payload_ref, lambda slot: ghosts_ref.at[slot], send_sem, recv_sem
    )
    each_slot(start)
    each_slot(wait)


def second_kernel(
    count_ref,
    target_ref,
    from_ref,
    group_ref,
    source_ref,
    own_ref,
    ghosts_ref,
    table_ref,
    cell_ref,
    offset_ref,
    force_ref,
    dest_ref,
    moved_ref,
    leaving_ref,
    centre_ref,
    places,
    sides,
    targets,
    near,
    values,
    sums,
    chosen,
):
    for group in range(GROUPS):
        for row in range(3):
            places[pl.ds(group * 64 + 8 * row, 8), :] = own_ref[group, row]

    def spread(slot, carry):
        at = pl.multiple_of((GROUPS + slot) * 64, 64)
        for row in range(3):
            places[pl.ds(at + 8 * row, 8), :] = ghosts_ref[slot, row]
        return carry

    lax.fori_loop(0, 27, spread, 0)
    near_pass(
        1, count_ref, target_ref, from_ref, group_ref, source_ref, places, sides, targets, near, chosen
    )
    for group in range(GROUPS):
        offsets = [offset_ref[group, row] for row in range(3)]
        forces = forces_of(group, offsets, cell_ref, source_ref, table_ref, near)
        for row in range(3):
            moved = offsets[row] + STEP_SIZE * forces[row]
            half = 0.5 * (force_ref[group, row] + forces[row])
            for tile in range(8):
                lanes = pl.ds((8 * group + tile) * TILE, TILE)
                moved_ref[pl.ds(row, 1), lanes] = moved[tile : tile + 1]
                values[pl.ds(row, 1), lanes] = half[tile : tile + 1]
    sums[...] = jnp.zeros(sums.shape, F32)
    width = 512
    high_ids = lax.broadcasted_iota(jnp.int32, (128, width), 0)
    low_ids = lax.broadcasted_iota(jnp.int32, (256, width), 0)

    def scatter(block, carry):
        lanes = pl.ds(pl.multiple_of(block * width, width), width)
        parts = [halves_of(values[pl.ds(row, 1), lanes]) for row in range(3)]
        for end in range(2):
            dest = dest_ref[pl.ds(end, 1), lanes]
            node = dest & (SEG - 1)
            slot = dest >> 12
            upper = jnp.where(slot == 13, 0, 16 + 4 * slot) + (node >> 8)
            lower = node & 255
            chosen_rows = high_ids == upper
            left = jnp.concatenate(
                [
                    jnp.where(chosen_rows, parts[row][piece], 0.0).astype(BF16)
                    for row in range(3)
                    for piece in range(2)
                ],
                axis=0,
            )
            right = jnp.where(low_ids == lower, 1.0, 0.0).astype(BF16)
            sums[...] += lax.dot_general(left, right, NT, preferred_element_type=F32)
        return carry

    lax.fori_loop(0, SEG // width, scatter, 0)
    for row in range(3):
        at = 256 * row
        centre_ref[row] = sums[pl.ds(at, 16), :] + sums[pl.ds(at + 128, 16), :]
        for slot in range(27):
            both = sums[pl.ds(at + 16 + 4 * slot, 4), :] + sums[pl.ds(at + 144 + 4 * slot, 4), :]
            leaving_ref[slot, row, pl.ds(0, 4), :] = both[:, :TILE]
            leaving_ref[slot, row, pl.ds(4, 4), :] = both[:, TILE:]


def nodes_kernel(sizes, leaving_ref, centre_ref, out_ref, landed, send_sem, recv_sem):
    place = Place(sizes)
    barrier = pltpu.get_barrier_semaphore()
    greet_neighbours(place, barrier)

    def clear(slot):
        _, inside = place.beside(slot)

        @pl.when(jnp.logical_not(inside))
        def _():
            landed[slot] = jnp.zeros((3, 8, TILE), F32)

    each_slot(clear)
    pl.semaphore_wait(barrier, place.count_beside())
    start, wait = exchange(
        place, lambda slot: leaving_ref.at[slot], lambda slot: landed.at[slot], send_sem, recv_sem
    )
    each_slot(start)
    for row in range(3):
        for part in range(4, 16):
            out_ref[pl.ds(row, 1), pl.ds(256 * part, 256)] = centre_ref[row, pl.ds(part, 1), :]
    each_slot(wait)
    for row in range(3):
        total = landed[0, row]
        for slot in range(1, 27):
            total = total + landed[slot, row]
        for part in range(4):
            for half in range(2):
                lanes = slice(TILE * half, TILE * half + TILE)
                out_ref[pl.ds(row, 1), pl.ds(256 * part + TILE * half, TILE)] = (
                    centre_ref[row, pl.ds(part, 1), lanes]
                    + total[4 * half + part : 4 * half + part + 1]
                )


def on_device(
    sizes,
    seg_rel,
    burgers,
    line_vec,
    seg_cell,
    ghost_tiles,
    ghost_count,
    pair_target,
    pair_source,
    pair_group,
    pair_count,
    node_dest,
):
    nx, ny, nz = sizes
    plane = ny * nz
    cell = seg_cell.reshape(SEG // TILE, TILE)
    shape = jax.ShapeDtypeStruct
    dma = pltpu.SemaphoreType.DMA
    source, base, table = pl.pallas_call(
        functools.partial(expand_kernel, sizes),
        out_shape=(
            shape((GROUPS + 27, 9, 8, TILE), F32),
            shape((GROUPS, 3, 8, TILE), F32),
            shape((2 * TILE, TILE), F32),
        ),
        in_specs=vmem(4) + smem(2),
        out_specs=tuple(vmem(3)),
        scratch_shapes=[
            pltpu.VMEM((GROUPS, 9, 8, TILE), F32),
            pltpu.VMEM((9, GHOST_DEV, TILE), F32),
            pltpu.VMEM((40 * 32, TILE), F32),
            pltpu.VMEM((COMP * 32, TILE), F32),
            pltpu.VMEM((plane * CELL_DEV, 2 * TILE), F32),
            pltpu.VMEM((nx * CELL_DEV, 2 * TILE), F32),
            pltpu.VMEM((nx, CELL_DEV, 2 * TILE), F32),
            dma((27,)),
            dma((27,)),
            dma((plane,)),
            dma((plane,)),
            dma((nx,)),
            dma((nx,)),
        ],
        compiler_params=pltpu.CompilerParams(
            collective_id=0, has_side_effects=True, vmem_limit_bytes=32 << 20
        ),
        name="expand",
    )(seg_rel, burgers, line_vec, cell, ghost_tiles, ghost_count)
    near_scratch = [
        pltpu.VMEM(((GROUPS + 27) * 64, TILE), F32),
        pltpu.VMEM(((GROUPS + 27) * 256, TILE), F32),
        pltpu.VMEM((GROUPS * 256, TILE), F32),
        pltpu.VMEM((GROUPS * 24, TILE), F32),
    ]
    own_shape = shape((GROUPS, 3, 8, TILE), F32)
    offset, force, own, payload = pl.pallas_call(
        first_kernel,
        out_shape=(own_shape, own_shape, own_shape, shape((3, GHOST_DEV, TILE), F32)),
        in_specs=smem(5) + vmem(5),
        out_specs=tuple(vmem(4)),
        scratch_shapes=near_scratch + [pltpu.SMEM((PAIRS,), jnp.int32)],
        compiler_params=pltpu.CompilerParams(vmem_limit_bytes=32 << 20),
        name="first",
    )(
        pair_count,
        pair_target,
        pair_source,
        pair_group,
        ghost_tiles,
        source,
        base,
        table,
        cell,
        seg_rel,
    )
    ghosts = pl.pallas_call(
        functools.partial(ghosts_kernel, sizes),
        out_shape=shape((27, 3, GHOST_DEV, TILE), F32),
        in_specs=vmem(1),
        out_specs=vmem(1)[0],
        scratch_shapes=[dma((27,)), dma((27,))],
        compiler_params=pltpu.CompilerParams(collective_id=1, has_side_effects=True),
        name="ghosts",
    )(payload)
    moved, leaving, centre = pl.pallas_call(
        second_kernel,
        out_shape=(
            shape((3, SEG), F32),
            shape((27, 3, 8, TILE), F32),
            shape((3, 16, 2 * TILE), F32),
        ),
        in_specs=smem(4) + vmem(8),
        out_specs=tuple(vmem(3)),
        scratch_shapes=near_scratch
        + [
            pltpu.VMEM((8, SEG), F32),
            pltpu.VMEM((768, 256), F32),
            pltpu.SMEM((PAIRS,), jnp.int32),
        ],
        compiler_params=pltpu.CompilerParams(vmem_limit_bytes=32 << 20),
        name="second",
    )(
        pair_count,
        pair_target,
        pair_source,
        pair_group,
        source,
        own,
        ghosts,
        table,
        cell,
        offset,
        force,
        node_dest,
    )
    nodes = pl.pallas_call(
        functools.partial(nodes_kernel, sizes),
        out_shape=shape((3, SEG), F32),
        in_specs=vmem(2),
        out_specs=vmem(1)[0],
        scratch_shapes=[pltpu.VMEM((27, 3, 8, TILE), F32), dma((27,)), dma((27,))],
        compiler_params=pltpu.CompilerParams(collective_id=2, has_side_effects=True),
        name="nodes",
    )(leaving, centre)
    return moved, nodes


def solution(mesh):
    sizes = tuple(mesh.shape[name] for name in ("gx", "gy", "gz"))
    whole = ("gx", "gy", "gz")
    return jax.shard_map(
        functools.partial(on_device, sizes),
        mesh=mesh,
        in_specs=(P(None, whole),) * 3 + (P(whole),) * 7 + (P(None, whole),),
        out_specs=(P(None, whole), P(None, whole)),
        check_vma=False,
    )
```

```python
import functools

import jax
import jax.numpy as jnp
from jax import lax
from jax.experimental import pallas as pl
from jax.experimental.pallas import tpu as pltpu
from jax.sharding import PartitionSpec as P

TILE = 128
SEG = 4096
GROUPS = 4
GHOST_DEV = 8
CELL_DEV = 16
COMP = 6
TERMS = 35
LANE_STEP = 42
PAIRS = 128
CORE2 = 0.25
NEAR_SCALE = 0.05
FAR_SCALE = 0.002
STEP_SIZE = 0.1
MESH = pl.DeviceIdType.MESH
F32 = jnp.float32
BF16 = jnp.bfloat16
EXPONENTS = [
    (a, b, degree - a - b)
    for degree in range(5)
    for a in range(degree, -1, -1)
    for b in range(degree - a, -1, -1)
]
NT = (((1,), (1,)), ((), ()))
TN = (((0,), (0,)), ((), ()))


def vmem(count):
    return [pl.BlockSpec(memory_space=pltpu.VMEM)] * count


def smem(count):
    return [pl.BlockSpec(memory_space=pltpu.SMEM)] * count


def halves_of(value):
    high = value.astype(BF16).astype(F32)
    return high, value - high


def powers(unit):
    square = unit * unit
    return [None, unit, square, square * unit, square * square]


def monomial(u, v, w, exps):
    result = None
    for table, power in zip((u, v, w), exps):
        if power:
            result = table[power] if result is None else result * table[power]
    return result


def symmetric(b, t):
    return [
        b[0] * t[0],
        b[1] * t[1],
        b[2] * t[2],
        0.5 * (b[0] * t[1] + b[1] * t[0]),
        0.5 * (b[1] * t[2] + b[2] * t[1]),
        0.5 * (b[0] * t[2] + b[2] * t[0]),
    ]


class Place:
    def __init__(self, sizes):
        self.sizes = sizes
        self.at = tuple(lax.axis_index(name) for name in ("gx", "gy", "gz"))

    def beside(self, slot, sign=1):
        steps = (slot // 9 - 1, slot // 3 % 3 - 1, slot % 3 - 1)
        where = tuple(a + sign * s for a, s in zip(self.at, steps))
        inside = slot != 13
        for at, size in zip(where, self.sizes):
            inside = jnp.logical_and(inside, jnp.logical_and(at >= 0, at < size))
        return where, inside

    def count_beside(self):
        total = 1
        for at, size in zip(self.at, self.sizes):
            total = total * (3 - (at == 0).astype(jnp.int32) - (at == size - 1).astype(jnp.int32))
        return total - 1


def each_slot(body):
    def step(slot, carry):
        body(slot)
        return carry

    lax.fori_loop(0, 27, step, 0)


def greet_neighbours(place, barrier):
    def greet(slot):
        where, inside = place.beside(slot)

        @pl.when(inside)
        def _():
            pl.semaphore_signal(barrier, inc=1, device_id=where, device_id_type=MESH)

    each_slot(greet)


def far_force(offset, burg, line, cell, table_ref):
    u, v, w = (powers(2.0 * value) for value in offset)
    stress = [None] * COMP
    for at, exps in enumerate(EXPONENTS):
        value = monomial(u, v, w, exps)
        for comp in range(COMP):
            row = comp // 3 * TILE + comp % 3 * LANE_STEP + at
            entry = jnp.broadcast_to(table_ref[pl.ds(row, 1), :], (8, TILE))
            term = jnp.take_along_axis(entry, cell, axis=1, mode="promise_in_bounds")
            if value is not None:
                term = term * value
            stress[comp] = term if stress[comp] is None else stress[comp] + term
    push_x = stress[0] * burg[0] + stress[3] * burg[1] + stress[5] * burg[2]
    push_y = stress[3] * burg[0] + stress[1] * burg[1] + stress[4] * burg[2]
    push_z = stress[5] * burg[0] + stress[4] * burg[1] + stress[2] * burg[2]
    return [
        push_y * line[2] - push_z * line[1],
        push_z * line[0] - push_x * line[2],
        push_x * line[1] - push_y * line[0],
    ]


def exchange(place, send_of, receive_at, send_sem, recv_sem):
    def copy_of(slot):
        where, inside = place.beside(slot)
        copy = pltpu.make_async_remote_copy(
            src_ref=send_of(slot),
            dst_ref=receive_at(26 - slot),
            send_sem=send_sem.at[slot],
            recv_sem=recv_sem.at[26 - slot],
            device_id=where,
            device_id_type=MESH,
        )
        return copy, inside

    def start(slot):
        copy, inside = copy_of(slot)

        @pl.when(inside)
        def _():
            copy.start()

    def wait(slot):
        copy, inside = copy_of(slot)

        @pl.when(inside)
        def _():
            copy.wait_send()

        arriving, _ = copy_of(26 - slot)

        @pl.when(inside)
        def _():
            arriving.wait_recv()

    return start, wait


SIDE = 48 * 8
ACROSS = 80 * 8
UNROLL = 8
WIDTH = 512


def pieces_of(value):
    high = value.astype(BF16).astype(F32)
    rest = value - high
    middle = rest.astype(BF16).astype(F32)
    return [high, middle, rest - middle]


def product_halves(burg, line):
    highs, lows = [], []
    for b in burg:
        for t in line:
            high, low = halves_of(b * t)
            highs.append(high)
            lows.append(low)
    return highs, lows


def store_rows(ref, at, rows):
    for row, value in enumerate(rows):
        ref[pl.ds(at + 8 * row, 8), :] = value


def fill_strengths(sides, group, burg, line):
    highs, lows = product_halves(burg, line)
    zero, one = jnp.zeros((8, TILE), F32), jnp.ones((8, TILE), F32)
    at = pl.multiple_of(group * SIDE, SIDE)
    store_rows(sides, at, highs + highs + lows + [zero] * 5)
    store_rows(sides, at + 41 * 8, [one] * 3 + [zero] * 4)


def fill_places(sides, group, places):
    at = pl.multiple_of(group * SIDE, SIDE)
    store_rows(sides, at + 32 * 8, [piece for place in places for piece in pieces_of(place)])


def fill_across_strengths(across, group, burg, line):
    highs, lows = product_halves(burg, line)
    zero = jnp.zeros((8, TILE), F32)
    store_rows(across, group * ACROSS, highs + lows + highs + [zero] * 5)


def fill_across_places(across, group, places):
    zero, one = jnp.zeros((8, TILE), F32), jnp.ones((8, TILE), F32)
    for row in range(3):
        signs = [-one if at // 3 == row else zero for at in range(9)]
        store_rows(
            across,
            group * ACROSS + (32 + 16 * row) * 8,
            signs + pieces_of(places[row]) + [zero] * 4,
        )


def fill_targets(across, targets, strengths):
    def fill(tile, carry):
        at = tile // 8 * ACROSS + tile % 8
        if strengths:
            top = across[pl.ds(at, 32, stride=8), :]
            zero = jnp.zeros((32, 3 * TILE), F32)
            targets[tile, pl.ds(0, 32), :] = jnp.concatenate([top, zero], axis=1).astype(BF16)
        low = [across[pl.ds(at + (32 + 16 * row) * 8, 16, stride=8), :] for row in range(3)]
        low = jnp.concatenate([jnp.zeros((16, TILE), F32)] + low, axis=1)
        targets[tile, pl.ds(32, 16), :] = low.astype(BF16)
        return carry

    lax.fori_loop(0, SEG // TILE, fill, 0)


def near_pass(sweep, live, target_ref, from_ref, target_row, group_row, sides, targets, pairs, near):
    def forces_of_pair(pair):
        source = from_ref[pair]
        left = sides[pl.ds((source >> 3) * SIDE + (source & 7), 48, stride=8), :]
        both = lax.dot_general(
            left.astype(BF16), targets[target_ref[pair]], TN, preferred_element_type=F32
        )
        totals = [jnp.zeros((8, TILE), F32)] * 3
        for chunk in range(16):
            span = both[8 * chunk : 8 * chunk + 8]
            gaps = [span[:, TILE * (row + 1) : TILE * (row + 2)] for row in range(3)]
            radius2 = gaps[0] * gaps[0] + gaps[1] * gaps[1] + gaps[2] * gaps[2] + CORE2
            inverse = lax.rsqrt(radius2)
            weight = span[:, :TILE] * (inverse * inverse * inverse)
            totals = [total + weight * gap for total, gap in zip(totals, gaps)]
        return totals

    def step(block, carry):
        results = [forces_of_pair(block * UNROLL + at) for at in range(UNROLL)]
        for row in range(3):
            rows = [jnp.sum(totals[row], axis=0, keepdims=True) for totals in results]
            at = pl.multiple_of(row * PAIRS + block * UNROLL, UNROLL)
            pairs[pl.ds(at, UNROLL), :] = jnp.concatenate(rows, axis=0)
        return carry

    lax.fori_loop(0, PAIRS // UNROLL, step, 0)
    tile_ids = lax.broadcasted_iota(jnp.int32, (SEG // TILE, PAIRS), 0)
    pair_ids = lax.broadcasted_iota(jnp.int32, (SEG // TILE, PAIRS), 1)
    wanted = (tile_ids == target_row) & (group_row == sweep) & (pair_ids < live)
    select = jnp.where(wanted, 1.0, 0.0).astype(BF16)
    for row in range(3):
        total = None
        for piece in pieces_of(pairs[pl.ds(row * PAIRS, PAIRS), :]):
            part = jnp.dot(select, piece.astype(BF16), preferred_element_type=F32)
            total = part if total is None else total + part
        near[pl.ds(32 * row, 32), :] = total


def step_kernel(
    sizes,
    ghost_ref,
    live_ref,
    count_ref,
    target_ref,
    from_ref,
    rel_hbm,
    burg_hbm,
    line_hbm,
    cell_hbm,
    dest_hbm,
    target_hbm,
    group_hbm,
    moved_ref,
    nodes_ref,
    rel_ref,
    burg_ref,
    line_ref,
    cell_ref,
    dest_ref,
    target_row,
    group_row,
    own,
    base,
    offset,
    force,
    far,
    payload,
    landing,
    payload_next,
    landing_next,
    mono,
    symm,
    gathered,
    contrib,
    arrived,
    table_ref,
    sides,
    across,
    targets,
    pairs,
    near,
    values,
    lowers,
    centre,
    sums,
    leaving,
    landed,
    load_sem,
    ghost_send,
    ghost_recv,
    next_send,
    next_recv,
    node_send,
    node_recv,
    plane_send,
    plane_recv,
    line_send,
    line_recv,
):
    loads = [
        pltpu.make_async_copy(source, target, load_sem.at[at])
        for at, (source, target) in enumerate(
            [
                (rel_hbm, rel_ref),
                (burg_hbm, burg_ref),
                (line_hbm, line_ref),
                (cell_hbm, cell_ref),
                (dest_hbm, dest_ref),
                (target_hbm, target_row),
                (group_hbm, group_row),
            ]
        )
    ]
    for load in loads:
        load.start()
    nx, ny, nz = sizes
    plane = ny * nz
    place = Place(sizes)
    gx, gy, gz = place.at
    here = gy * nz + gz

    def plane_peer(step):
        peer = lax.rem(here + step, plane)
        return (gx, peer // nz, lax.rem(peer, nz))

    def line_peer(step):
        return (lax.rem(gx + step, nx), gy, gz)

    barrier = pltpu.get_barrier_semaphore()
    greet_neighbours(place, barrier)

    def greet_plane(step, carry):
        pl.semaphore_signal(barrier, inc=1, device_id=plane_peer(step), device_id_type=MESH)
        return carry

    def greet_line(step, carry):
        pl.semaphore_signal(barrier, inc=1, device_id=line_peer(step), device_id_type=MESH)
        return carry

    lax.fori_loop(1, plane, greet_plane, 0)
    lax.fori_loop(1, nx, greet_line, 0)

    for load in loads:
        load.wait()
    for tile in range(SEG // TILE):
        lanes = pl.ds(tile * TILE, TILE)
        for row in range(3):
            own[tile // 8, row, pl.ds(tile % 8, 1), :] = rel_ref[pl.ds(row, 1), lanes]
            own[tile // 8, 3 + row, pl.ds(tile % 8, 1), :] = burg_ref[pl.ds(row, 1), lanes]
            own[tile // 8, 6 + row, pl.ds(tile % 8, 1), :] = line_ref[pl.ds(row, 1), lanes]
    for group in range(GROUPS):
        rows = slice(8 * group, 8 * group + 8)
        cell = cell_ref[rows, :]
        rel = [own[group, row] for row in range(3)]
        burg = [own[group, 3 + row] for row in range(3)]
        line = [own[group, 6 + row] for row in range(3)]
        corner = (
            jnp.full((8, TILE), gx, jnp.int32),
            gy * 4 + (cell >> 2),
            gz * 4 + (cell & 3),
        )
        for row in range(3):
            corner_row = corner[row].astype(F32) + 0.5
            base[group, row] = corner_row
            offset[group, row] = rel[row]
            own[group, row] = corner_row + rel[row]
        for at, value in enumerate(symmetric(burg, line)):
            symm[pl.ds(at * 32 + 8 * group, 8), :] = value
        u, v, w = (powers(2.0 * value) for value in rel)
        for at, exps in enumerate(EXPONENTS):
            value = monomial(u, v, w, exps)
            mono[pl.ds(at * 32 + 8 * group, 8), :] = (
                jnp.ones((8, TILE), F32) if value is None else value
            )
    for at in range(TERMS, 40):
        mono[pl.ds(at * 32, 32), :] = jnp.zeros((32, TILE), F32)
    for ghost in range(GHOST_DEV):
        tile = ghost_ref[ghost]
        live = jnp.where(ghost < live_ref[0], 1.0, 0.0)
        for row in range(9):
            value = own[tile // 8, row, pl.ds(lax.rem(tile, 8), 1), :]
            payload[row, pl.ds(ghost, 1), :] = value * live

    cells = lax.broadcasted_iota(jnp.int32, (CELL_DEV, TILE), 0)
    moments = jnp.zeros((COMP * CELL_DEV, 40), F32)
    for block in range(4):
        lefts, rights = [], []
        for tile in range(8 * block, 8 * block + 8):
            chosen = cells == cell_ref[pl.ds(tile, 1), :]
            left = jnp.concatenate(
                [
                    jnp.where(chosen, symm[pl.ds(at * 32 + tile, 1), :], 0.0)
                    for at in range(COMP)
                ],
                axis=0,
            )
            right = mono[pl.ds(tile, 40, stride=32), :]
            left_high, left_low = halves_of(left)
            right_high, right_low = halves_of(right)
            lefts += [left_high, left_high, left_low]
            rights += [right_high, right_low, right_high]
        moments = moments + lax.dot_general(
            jnp.concatenate(lefts, axis=1).astype(BF16),
            jnp.concatenate(rights, axis=1).astype(BF16),
            NT,
            preferred_element_type=F32,
        )
    wide = jnp.concatenate([moments, jnp.zeros((COMP * CELL_DEV, TILE - 40), F32)], axis=1)
    mine = pl.ds(pl.multiple_of(here * CELL_DEV, CELL_DEV), CELL_DEV)
    for half in range(2):
        total = jnp.zeros((CELL_DEV, TILE), F32)
        for third in range(3):
            at = (3 * half + third) * CELL_DEV
            part = wide[at : at + CELL_DEV]
            total = total + (pltpu.roll(part, third * LANE_STEP, 1) if third else part)
        gathered[mine, pl.ds(half * TILE, TILE)] = total

    pl.semaphore_wait(barrier, place.count_beside() + plane - 1 + nx - 1)

    def plane_copy(step):
        return pltpu.make_async_remote_copy(
            src_ref=gathered.at[mine],
            dst_ref=gathered.at[mine],
            send_sem=plane_send.at[step],
            recv_sem=plane_recv.at[step],
            device_id=plane_peer(step),
            device_id_type=MESH,
        )

    def ghost_copy(slot):
        where, inside = place.beside(slot)
        copy = pltpu.make_async_remote_copy(
            src_ref=payload,
            dst_ref=landing.at[26 - slot],
            send_sem=ghost_send.at[slot],
            recv_sem=ghost_recv.at[26 - slot],
            device_id=where,
            device_id_type=MESH,
        )
        return copy, inside

    def start_plane(step, carry):
        plane_copy(step).start()
        return carry

    lax.fori_loop(1, plane, start_plane, 0)

    def start_ghost(slot):
        copy, inside = ghost_copy(slot)

        @pl.when(inside)
        def _():
            copy.start()

    each_slot(start_ghost)

    def clear(slot):
        _, inside = place.beside(slot)

        @pl.when(jnp.logical_not(inside))
        def _():
            landed[slot] = jnp.zeros((3, 8, TILE), F32)

    each_slot(clear)

    for group in range(GROUPS):
        places = [own[group, row] for row in range(3)]
        burg = [own[group, 3 + row] for row in range(3)]
        line = [own[group, 6 + row] for row in range(3)]
        fill_strengths(sides, group, burg, line)
        fill_places(sides, group, places)
        fill_across_strengths(across, group, burg, line)
        fill_across_places(across, group, places)
    fill_targets(across, targets, True)
    rows, columns = nx * CELL_DEV, plane * CELL_DEV
    row = lax.broadcasted_iota(jnp.int32, (rows, columns), 0)
    column = lax.broadcasted_iota(jnp.int32, (rows, columns), 1)
    peer = column >> 4
    step_x = (row >> 4) - gx
    step_y = gy * 4 + ((row >> 2) & 3) - (peer // nz * 4 + ((column >> 2) & 3))
    step_z = gz * 4 + (row & 3) - (peer % nz * 4 + (column & 3))
    distance2 = (step_x * step_x + step_y * step_y + step_z * step_z).astype(F32)
    weight = jnp.where(distance2 > 3.5, 1.0 / jnp.sqrt(jnp.maximum(distance2, 1.0)), 0.0)

    def wait_plane(step, carry):
        plane_copy(step).wait()
        return carry

    lax.fori_loop(1, plane, wait_plane, 0)
    contrib[...] = jnp.dot(
        weight, gathered[...], precision=lax.Precision.HIGHEST, preferred_element_type=F32
    )

    def line_copy(step):
        there = lax.rem(gx + step, nx)
        return pltpu.make_async_remote_copy(
            src_ref=contrib.at[pl.ds(pl.multiple_of(there * CELL_DEV, CELL_DEV), CELL_DEV)],
            dst_ref=arrived.at[step],
            send_sem=line_send.at[step],
            recv_sem=line_recv.at[step],
            device_id=line_peer(step),
            device_id_type=MESH,
        )

    def start_line(step, carry):
        line_copy(step).start()
        return carry

    lax.fori_loop(1, nx, start_line, 0)
    def take_ghosts(slot):
        copy, _ = ghost_copy(26 - slot)
        _, inside = place.beside(slot)

        @pl.when(inside)
        def _():
            copy.wait_recv()
            block = [landing[slot, row] for row in range(9)]
            fill_strengths(sides, GROUPS + slot, block[3:6], block[6:9])
            fill_places(sides, GROUPS + slot, block[0:3])

        @pl.when(jnp.logical_not(inside))
        def _():
            nothing = [jnp.zeros((8, TILE), F32)] * 3
            fill_strengths(sides, GROUPS + slot, nothing, nothing)
            fill_places(sides, GROUPS + slot, nothing)

    each_slot(take_ghosts)
    live = count_ref[0]
    near_pass(
        0, live, target_ref, from_ref, target_row[...], group_row[...], sides, targets, pairs, near
    )
    total = contrib[pl.ds(pl.multiple_of(gx * CELL_DEV, CELL_DEV), CELL_DEV), :]

    def wait_line(step, carry):
        line_copy(step).wait()
        return carry

    lax.fori_loop(1, nx, wait_line, 0)
    for step in range(1, nx):
        total = total + arrived[step]
    full = jnp.concatenate([total, jnp.zeros((TILE - CELL_DEV, 2 * TILE), F32)], axis=0)
    table_ref[pl.ds(0, TILE), :] = full[:, :TILE].T
    table_ref[pl.ds(TILE, TILE), :] = full[:, TILE:].T
    def far_pass(group):
        return far_force(
            [offset[group, row] for row in range(3)],
            [own[group, 3 + row] for row in range(3)],
            [own[group, 6 + row] for row in range(3)],
            cell_ref[pl.ds(8 * group, 8), :],
            table_ref,
        )

    for group in range(GROUPS):
        coupling = far_pass(group)
        for row in range(3):
            total = FAR_SCALE * coupling[row] + NEAR_SCALE * near[pl.ds(32 * row + 8 * group, 8), :]
            moved = offset[group, row] + STEP_SIZE * total
            force[group, row] = total
            offset[group, row] = moved
            own[group, row] = base[group, row] + moved
    for ghost in range(GHOST_DEV):
        tile = ghost_ref[ghost]
        for row in range(3):
            payload_next[row, pl.ds(ghost, 1), :] = own[tile // 8, row, pl.ds(lax.rem(tile, 8), 1), :]
    start_next, wait_next = exchange(
        place, lambda slot: payload_next, lambda slot: landing_next.at[slot], next_send, next_recv
    )
    each_slot(start_next)

    for group in range(GROUPS):
        coupling = far_pass(group)
        for row in range(3):
            far[group, row] = coupling[row]
        places = [own[group, row] for row in range(3)]
        fill_places(sides, group, places)
        fill_across_places(across, group, places)
    fill_targets(across, targets, False)
    low_ids = lax.broadcasted_iota(jnp.int32, (256, WIDTH), 0)

    def fill_lowers(block, carry):
        lanes = pl.ds(pl.multiple_of(block * WIDTH, WIDTH), WIDTH)
        for end in range(2):
            lower = dest_ref[pl.ds(end, 1), lanes] & 255
            lowers[block, end] = jnp.where(low_ids == lower, 1.0, 0.0).astype(BF16)
        return carry

    lax.fori_loop(0, SEG // WIDTH, fill_lowers, 0)

    def take_next(slot):
        wait_next(slot)
        _, inside = place.beside(slot)

        @pl.when(inside)
        def _():
            fill_places(sides, GROUPS + slot, [landing_next[slot, row] for row in range(3)])

    each_slot(take_next)
    near_pass(
        1, live, target_ref, from_ref, target_row[...], group_row[...], sides, targets, pairs, near
    )
    for group in range(GROUPS):
        for row in range(3):
            total = FAR_SCALE * far[group, row] + NEAR_SCALE * near[pl.ds(32 * row + 8 * group, 8), :]
            moved = offset[group, row] + STEP_SIZE * total
            half = 0.5 * (force[group, row] + total)
            for tile in range(8):
                lanes = pl.ds((8 * group + tile) * TILE, TILE)
                moved_ref[pl.ds(row, 1), lanes] = moved[tile : tile + 1]
                values[pl.ds(row, 1), lanes] = half[tile : tile + 1]

    def scatter(first, count, totals):
        totals[...] = jnp.zeros(totals.shape, F32)
        high_ids = lax.broadcasted_iota(jnp.int32, (count, WIDTH), 0) + first

        def add(block, carry):
            lanes = pl.ds(pl.multiple_of(block * WIDTH, WIDTH), WIDTH)
            parts = [halves_of(values[pl.ds(row, 1), lanes]) for row in range(3)]
            for end in range(2):
                dest = dest_ref[pl.ds(end, 1), lanes]
                slot = dest >> 12
                upper = jnp.where(slot == 13, 0, 16 + 4 * slot) + ((dest & (SEG - 1)) >> 8)
                chosen = high_ids == upper
                left = jnp.concatenate(
                    [
                        jnp.where(chosen, parts[row][piece], 0.0).astype(BF16)
                        for row in range(3)
                        for piece in range(2)
                    ],
                    axis=0,
                )
                totals[...] += lax.dot_general(
                    left, lowers[block, end], NT, preferred_element_type=F32
                )
            return carry

        lax.fori_loop(0, SEG // WIDTH, add, 0)

    scatter(16, 112, sums)
    for row in range(3):
        for slot in range(27):
            at = 224 * row + 4 * slot
            both = sums[pl.ds(at, 4), :] + sums[pl.ds(at + 112, 4), :]
            leaving[slot, row, pl.ds(0, 4), :] = both[:, :TILE]
            leaving[slot, row, pl.ds(4, 4), :] = both[:, TILE:]
    start_node, wait_node = exchange(
        place, lambda slot: leaving.at[slot], lambda slot: landed.at[slot], node_send, node_recv
    )
    each_slot(start_node)
    scatter(0, 16, centre)
    middle = [
        centre[pl.ds(32 * row, 16), :] + centre[pl.ds(32 * row + 16, 16), :] for row in range(3)
    ]
    for row in range(3):
        for part in range(4, 16):
            nodes_ref[pl.ds(row, 1), pl.ds(256 * part, 256)] = middle[row][part : part + 1]
    each_slot(wait_node)
    for row in range(3):
        total = landed[0, row]
        for slot in range(1, 27):
            total = total + landed[slot, row]
        for part in range(4):
            for half in range(2):
                lanes = slice(TILE * half, TILE * half + TILE)
                nodes_ref[pl.ds(row, 1), pl.ds(256 * part + TILE * half, TILE)] = (
                    middle[row][part : part + 1, lanes]
                    + total[4 * half + part : 4 * half + part + 1]
                )

    def wait_ghost_send(slot):
        copy, inside = ghost_copy(slot)

        @pl.when(inside)
        def _():
            copy.wait_send()

    each_slot(wait_ghost_send)


def on_device(
    sizes,
    seg_rel,
    burgers,
    line_vec,
    seg_cell,
    ghost_tiles,
    ghost_count,
    pair_target,
    pair_source,
    pair_group,
    pair_count,
    node_dest,
):
    nx, ny, nz = sizes
    plane = ny * nz
    cell = seg_cell.reshape(SEG // TILE, TILE)
    shape = jax.ShapeDtypeStruct
    dma = pltpu.SemaphoreType.DMA
    block = (GROUPS, 3, 8, TILE)
    buffers = [
        (3, SEG),
        (3, SEG),
        (3, SEG),
        (SEG // TILE, TILE, jnp.int32),
        (2, SEG, jnp.int32),
        (1, PAIRS, jnp.int32),
        (1, PAIRS, jnp.int32),
        (GROUPS, 9, 8, TILE),
        block,
        block,
        block,
        block,
        (9, GHOST_DEV, TILE),
        (27, 9, GHOST_DEV, TILE),
        (3, GHOST_DEV, TILE),
        (27, 3, GHOST_DEV, TILE),
        (40 * 32, TILE),
        (COMP * 32, TILE),
        (plane * CELL_DEV, 2 * TILE),
        (nx * CELL_DEV, 2 * TILE),
        (nx, CELL_DEV, 2 * TILE),
        (2 * TILE, TILE),
        ((GROUPS + 27) * SIDE, TILE),
        (GROUPS * ACROSS, TILE),
        (SEG // TILE, 48, 4 * TILE, BF16),
        (3 * PAIRS, TILE),
        (3 * SEG // TILE, TILE),
        (8, SEG),
        (SEG // WIDTH, 2, 256, WIDTH, BF16),
        (96, 256),
        (672, 256),
        (27, 3, 8, TILE),
        (27, 3, 8, TILE),
    ]
    scratch = []
    for sides in buffers:
        kind = F32
        if not isinstance(sides[-1], int):
            sides, kind = sides[:-1], sides[-1]
        scratch.append(pltpu.VMEM(sides, kind))
    return pl.pallas_call(
        functools.partial(step_kernel, sizes),
        out_shape=(shape((3, SEG), F32), shape((3, SEG), F32)),
        in_specs=smem(5) + [pl.BlockSpec(memory_space=pl.ANY)] * 7,
        out_specs=tuple(vmem(2)),
        scratch_shapes=scratch
        + [dma((7,))]
        + [dma((27,))] * 6
        + [dma((plane,))] * 2
        + [dma((nx,))] * 2,
        compiler_params=pltpu.CompilerParams(
            collective_id=0, has_side_effects=True, vmem_limit_bytes=56 << 20
        ),
        name="step",
    )(
        ghost_tiles,
        ghost_count,
        pair_count,
        pair_target,
        pair_source,
        seg_rel,
        burgers,
        line_vec,
        cell,
        node_dest,
        pair_target.reshape(1, PAIRS),
        pair_group.reshape(1, PAIRS),
    )


def solution(mesh):
    sizes = tuple(mesh.shape[name] for name in ("gx", "gy", "gz"))
    whole = ("gx", "gy", "gz")
    return jax.shard_map(
        functools.partial(on_device, sizes),
        mesh=mesh,
        in_specs=(P(None, whole),) * 3 + (P(whole),) * 7 + (P(None, whole),),
        out_specs=(P(None, whole), P(None, whole)),
        check_vma=False,
    )
```

```python
import functools

import jax
import jax.numpy as jnp
from jax import lax
from jax.experimental import pallas as pl
from jax.experimental.pallas import tpu as pltpu
from jax.sharding import PartitionSpec as P

TILE = 128
SEG = 4096
GROUPS = 4
GHOST_DEV = 8
CELL_DEV = 16
COMP = 6
TERMS = 35
LANE_STEP = 42
PAIRS = 128
CORE2 = 0.25
NEAR_SCALE = 0.05
FAR_SCALE = 0.002
STEP_SIZE = 0.1
MESH = pl.DeviceIdType.MESH
F32 = jnp.float32
BF16 = jnp.bfloat16
EXPONENTS = [
    (a, b, degree - a - b)
    for degree in range(5)
    for a in range(degree, -1, -1)
    for b in range(degree - a, -1, -1)
]
NT = (((1,), (1,)), ((), ()))
TN = (((0,), (0,)), ((), ()))


def vmem(count):
    return [pl.BlockSpec(memory_space=pltpu.VMEM)] * count


def smem(count):
    return [pl.BlockSpec(memory_space=pltpu.SMEM)] * count


def halves_of(value):
    high = value.astype(BF16).astype(F32)
    return high, value - high


def powers(unit):
    square = unit * unit
    return [None, unit, square, square * unit, square * square]


def monomial(u, v, w, exps):
    result = None
    for table, power in zip((u, v, w), exps):
        if power:
            result = table[power] if result is None else result * table[power]
    return result


def symmetric(b, t):
    return [
        b[0] * t[0],
        b[1] * t[1],
        b[2] * t[2],
        0.5 * (b[0] * t[1] + b[1] * t[0]),
        0.5 * (b[1] * t[2] + b[2] * t[1]),
        0.5 * (b[0] * t[2] + b[2] * t[0]),
    ]


class Place:
    def __init__(self, sizes):
        self.sizes = sizes
        self.at = tuple(lax.axis_index(name) for name in ("gx", "gy", "gz"))
        self.free = [
            {-1: at > 0, 1: at < size - 1} for at, size in zip(self.at, sizes)
        ]

    def beside(self, slot):
        steps = (slot // 9 - 1, slot // 3 % 3 - 1, slot % 3 - 1)
        where = tuple(at + step for at, step in zip(self.at, steps))
        inside = None
        for free, step in zip(self.free, steps):
            if step:
                inside = free[step] if inside is None else jnp.logical_and(inside, free[step])
        return where, inside

    def count_beside(self):
        total = 1
        for at, size in zip(self.at, self.sizes):
            total = total * (3 - (at == 0).astype(jnp.int32) - (at == size - 1).astype(jnp.int32))
        return total - 1


def each_slot(body):
    for slot in range(27):
        if slot != 13:
            body(slot)


def greet_neighbours(place, barrier):
    def greet(slot):
        where, inside = place.beside(slot)

        @pl.when(inside)
        def _():
            pl.semaphore_signal(barrier, inc=1, device_id=where, device_id_type=MESH)

    each_slot(greet)


def far_force(offset, burg, line, cell, table_ref):
    u, v, w = (powers(2.0 * value) for value in offset)
    stress = [None] * COMP
    for at, exps in enumerate(EXPONENTS):
        value = monomial(u, v, w, exps)
        for comp in range(COMP):
            row = comp // 3 * TILE + comp % 3 * LANE_STEP + at
            entry = jnp.broadcast_to(table_ref[pl.ds(row, 1), :], (8, TILE))
            term = jnp.take_along_axis(entry, cell, axis=1, mode="promise_in_bounds")
            if value is not None:
                term = term * value
            stress[comp] = term if stress[comp] is None else stress[comp] + term
    push_x = stress[0] * burg[0] + stress[3] * burg[1] + stress[5] * burg[2]
    push_y = stress[3] * burg[0] + stress[1] * burg[1] + stress[4] * burg[2]
    push_z = stress[5] * burg[0] + stress[4] * burg[1] + stress[2] * burg[2]
    return [
        push_y * line[2] - push_z * line[1],
        push_z * line[0] - push_x * line[2],
        push_x * line[1] - push_y * line[0],
    ]


def exchange(place, send_of, receive_at, send_sem, recv_sem):
    def copy_of(slot):
        where, inside = place.beside(slot)
        copy = pltpu.make_async_remote_copy(
            src_ref=send_of(slot),
            dst_ref=receive_at(26 - slot),
            send_sem=send_sem.at[slot],
            recv_sem=recv_sem.at[26 - slot],
            device_id=where,
            device_id_type=MESH,
        )
        return copy, inside

    def start(slot):
        copy, inside = copy_of(slot)

        @pl.when(inside)
        def _():
            copy.start()

    def wait(slot):
        arriving, _ = copy_of(26 - slot)
        _, inside = place.beside(slot)

        @pl.when(inside)
        def _():
            arriving.wait_recv()

    def wait_sent(slot):
        copy, inside = copy_of(slot)

        @pl.when(inside)
        def _():
            copy.wait_send()

    return start, wait, wait_sent


SIDE = 48 * 8
ACROSS = 80 * 8
UNROLL = 16
WIDTH = 512


def pieces_of(value):
    high = value.astype(BF16).astype(F32)
    rest = value - high
    middle = rest.astype(BF16).astype(F32)
    return [high, middle, rest - middle]


def product_halves(burg, line):
    highs, lows = [], []
    for b in burg:
        for t in line:
            high, low = halves_of(b * t)
            highs.append(high)
            lows.append(low)
    return highs, lows


def store_rows(ref, at, rows):
    for row, value in enumerate(rows):
        ref[pl.ds(at + 8 * row, 8), :] = value


def fill_strengths(sides, group, burg, line):
    highs, lows = product_halves(burg, line)
    zero, one = jnp.zeros((8, TILE), F32), jnp.ones((8, TILE), F32)
    at = pl.multiple_of(group * SIDE, SIDE)
    store_rows(sides, at, highs + highs + lows + [zero] * 5)
    store_rows(sides, at + 41 * 8, [one] * 3 + [zero] * 4)


def fill_places(sides, group, places):
    at = pl.multiple_of(group * SIDE, SIDE)
    store_rows(sides, at + 32 * 8, [piece for place in places for piece in pieces_of(place)])


def fill_across_strengths(across, group, burg, line):
    highs, lows = product_halves(burg, line)
    zero = jnp.zeros((8, TILE), F32)
    store_rows(across, group * ACROSS, highs + lows + highs + [zero] * 5)


def fill_across_places(across, group, places):
    zero, one = jnp.zeros((8, TILE), F32), jnp.ones((8, TILE), F32)
    for row in range(3):
        signs = [-one if at // 3 == row else zero for at in range(9)]
        store_rows(
            across,
            group * ACROSS + (32 + 16 * row) * 8,
            signs + pieces_of(places[row]) + [zero] * 4,
        )


def fill_targets(across, targets, strengths):
    def fill(tile, carry):
        at = tile // 8 * ACROSS + tile % 8
        if strengths:
            top = across[pl.ds(at, 32, stride=8), :]
            zero = jnp.zeros((32, 3 * TILE), F32)
            targets[tile, pl.ds(0, 32), :] = jnp.concatenate([top, zero], axis=1).astype(BF16)
        low = [across[pl.ds(at + (32 + 16 * row) * 8, 16, stride=8), :] for row in range(3)]
        low = jnp.concatenate([jnp.zeros((16, TILE), F32)] + low, axis=1)
        targets[tile, pl.ds(32, 16), :] = low.astype(BF16)
        return carry

    lax.fori_loop(0, SEG // TILE, fill, 0)


def near_pass(sweep, live, target_ref, from_ref, target_row, group_row, sides, targets, pairs, near):
    def forces_of_pair(pair):
        source = from_ref[pair]
        left = sides[pl.ds((source >> 3) * SIDE + (source & 7), 48, stride=8), :]
        both = lax.dot_general(
            left.astype(BF16), targets[target_ref[pair]], TN, preferred_element_type=F32
        )
        totals = [jnp.zeros((8, TILE), F32)] * 3
        for chunk in range(16):
            span = both[8 * chunk : 8 * chunk + 8]
            gaps = [span[:, TILE * (row + 1) : TILE * (row + 2)] for row in range(3)]
            radius2 = gaps[0] * gaps[0] + gaps[1] * gaps[1] + gaps[2] * gaps[2] + CORE2
            inverse = lax.rsqrt(radius2)
            weight = span[:, :TILE] * (inverse * inverse * inverse)
            totals = [total + weight * gap for total, gap in zip(totals, gaps)]
        return totals

    def step(block, carry):
        results = [forces_of_pair(block * UNROLL + at) for at in range(UNROLL)]
        for row in range(3):
            rows = [jnp.sum(totals[row], axis=0, keepdims=True) for totals in results]
            at = pl.multiple_of(row * PAIRS + block * UNROLL, UNROLL)
            pairs[pl.ds(at, UNROLL), :] = jnp.concatenate(rows, axis=0)
        return carry

    lax.fori_loop(0, PAIRS // UNROLL, step, 0)
    tile_ids = lax.broadcasted_iota(jnp.int32, (SEG // TILE, PAIRS), 0)
    pair_ids = lax.broadcasted_iota(jnp.int32, (SEG // TILE, PAIRS), 1)
    wanted = (tile_ids == target_row) & (group_row == sweep) & (pair_ids < live)
    select = jnp.where(wanted, 1.0, 0.0).astype(BF16)
    for row in range(3):
        total = None
        for piece in pieces_of(pairs[pl.ds(row * PAIRS, PAIRS), :]):
            part = jnp.dot(select, piece.astype(BF16), preferred_element_type=F32)
            total = part if total is None else total + part
        near[pl.ds(32 * row, 32), :] = total


def step_kernel(
    sizes,
    ghost_ref,
    live_ref,
    count_ref,
    target_ref,
    from_ref,
    rel_hbm,
    burg_hbm,
    line_hbm,
    cell_hbm,
    dest_hbm,
    target_hbm,
    group_hbm,
    moved_ref,
    nodes_ref,
    rel_ref,
    burg_ref,
    line_ref,
    cell_ref,
    dest_ref,
    target_row,
    group_row,
    own,
    base,
    offset,
    force,
    far,
    payload,
    landing,
    payload_next,
    landing_next,
    mono,
    symm,
    gathered,
    contrib,
    arrived,
    table_ref,
    sides,
    across,
    targets,
    pairs,
    near,
    values,
    lowers,
    centre,
    sums,
    leaving,
    landed,
    load_sem,
    ghost_send,
    ghost_recv,
    next_send,
    next_recv,
    node_send,
    node_recv,
    plane_send,
    plane_recv,
    line_send,
    line_recv,
):
    loads = [
        pltpu.make_async_copy(source, target, load_sem.at[at])
        for at, (source, target) in enumerate(
            [
                (rel_hbm, rel_ref),
                (burg_hbm, burg_ref),
                (line_hbm, line_ref),
                (cell_hbm, cell_ref),
                (dest_hbm, dest_ref),
                (target_hbm, target_row),
                (group_hbm, group_row),
            ]
        )
    ]
    for load in loads:
        load.start()
    nx, ny, nz = sizes
    plane = ny * nz
    place = Place(sizes)
    gx, gy, gz = place.at
    here = gy * nz + gz

    def plane_peer(step):
        peer = here + step
        peer = jnp.where(peer >= plane, peer - plane, peer)
        row = sum((peer >= nz * at).astype(jnp.int32) for at in range(1, ny))
        return (gx, row, peer - nz * row)

    def line_peer(step):
        there = gx + step
        return (jnp.where(there >= nx, there - nx, there), gy, gz)

    barrier = pltpu.get_barrier_semaphore()
    greet_neighbours(place, barrier)

    def greet_plane(step, carry):
        pl.semaphore_signal(barrier, inc=1, device_id=plane_peer(step), device_id_type=MESH)
        return carry

    def greet_line(step, carry):
        pl.semaphore_signal(barrier, inc=1, device_id=line_peer(step), device_id_type=MESH)
        return carry

    lax.fori_loop(1, plane, greet_plane, 0)
    lax.fori_loop(1, nx, greet_line, 0)

    for load in loads:
        load.wait()
    for tile in range(SEG // TILE):
        lanes = pl.ds(tile * TILE, TILE)
        for row in range(3):
            own[tile // 8, row, pl.ds(tile % 8, 1), :] = rel_ref[pl.ds(row, 1), lanes]
            own[tile // 8, 3 + row, pl.ds(tile % 8, 1), :] = burg_ref[pl.ds(row, 1), lanes]
            own[tile // 8, 6 + row, pl.ds(tile % 8, 1), :] = line_ref[pl.ds(row, 1), lanes]
    for group in range(GROUPS):
        rows = slice(8 * group, 8 * group + 8)
        cell = cell_ref[rows, :]
        rel = [own[group, row] for row in range(3)]
        burg = [own[group, 3 + row] for row in range(3)]
        line = [own[group, 6 + row] for row in range(3)]
        corner = (
            jnp.full((8, TILE), gx, jnp.int32),
            gy * 4 + (cell >> 2),
            gz * 4 + (cell & 3),
        )
        for row in range(3):
            corner_row = corner[row].astype(F32) + 0.5
            base[group, row] = corner_row
            offset[group, row] = rel[row]
            own[group, row] = corner_row + rel[row]
        for at, value in enumerate(symmetric(burg, line)):
            symm[pl.ds(at * 32 + 8 * group, 8), :] = value
        u, v, w = (powers(2.0 * value) for value in rel)
        for at, exps in enumerate(EXPONENTS):
            value = monomial(u, v, w, exps)
            mono[pl.ds(at * 32 + 8 * group, 8), :] = (
                jnp.ones((8, TILE), F32) if value is None else value
            )
    for at in range(TERMS, 40):
        mono[pl.ds(at * 32, 32), :] = jnp.zeros((32, TILE), F32)
    for ghost in range(GHOST_DEV):
        tile = ghost_ref[ghost]
        live = jnp.where(ghost < live_ref[0], 1.0, 0.0)
        for row in range(9):
            value = own[tile // 8, row, pl.ds(lax.rem(tile, 8), 1), :]
            payload[row, pl.ds(ghost, 1), :] = value * live

    cells = lax.broadcasted_iota(jnp.int32, (CELL_DEV, TILE), 0)
    moments = jnp.zeros((COMP * CELL_DEV, 40), F32)
    for block in range(4):
        lefts, rights = [], []
        for tile in range(8 * block, 8 * block + 8):
            chosen = cells == cell_ref[pl.ds(tile, 1), :]
            left = jnp.concatenate(
                [
                    jnp.where(chosen, symm[pl.ds(at * 32 + tile, 1), :], 0.0)
                    for at in range(COMP)
                ],
                axis=0,
            )
            right = mono[pl.ds(tile, 40, stride=32), :]
            left_high, left_low = halves_of(left)
            right_high, right_low = halves_of(right)
            lefts += [left_high, left_high, left_low]
            rights += [right_high, right_low, right_high]
        moments = moments + lax.dot_general(
            jnp.concatenate(lefts, axis=1).astype(BF16),
            jnp.concatenate(rights, axis=1).astype(BF16),
            NT,
            preferred_element_type=F32,
        )
    wide = jnp.concatenate([moments, jnp.zeros((COMP * CELL_DEV, TILE - 40), F32)], axis=1)
    mine = pl.ds(pl.multiple_of(here * CELL_DEV, CELL_DEV), CELL_DEV)
    for half in range(2):
        total = jnp.zeros((CELL_DEV, TILE), F32)
        for third in range(3):
            at = (3 * half + third) * CELL_DEV
            part = wide[at : at + CELL_DEV]
            total = total + (pltpu.roll(part, third * LANE_STEP, 1) if third else part)
        gathered[mine, pl.ds(half * TILE, TILE)] = total

    pl.semaphore_wait(barrier, place.count_beside() + plane - 1 + nx - 1)

    def plane_copy(step):
        return pltpu.make_async_remote_copy(
            src_ref=gathered.at[mine],
            dst_ref=gathered.at[mine],
            send_sem=plane_send.at[step],
            recv_sem=plane_recv.at[step],
            device_id=plane_peer(step),
            device_id_type=MESH,
        )

    def ghost_copy(slot):
        where, inside = place.beside(slot)
        copy = pltpu.make_async_remote_copy(
            src_ref=payload,
            dst_ref=landing.at[26 - slot],
            send_sem=ghost_send.at[slot],
            recv_sem=ghost_recv.at[26 - slot],
            device_id=where,
            device_id_type=MESH,
        )
        return copy, inside

    def start_plane(step, carry):
        plane_copy(step).start()
        return carry

    lax.fori_loop(1, plane, start_plane, 0)

    def start_ghost(slot):
        copy, inside = ghost_copy(slot)

        @pl.when(inside)
        def _():
            copy.start()

    each_slot(start_ghost)

    def clear(slot):
        _, inside = place.beside(slot)

        @pl.when(jnp.logical_not(inside))
        def _():
            landing[slot] = jnp.zeros((9, GHOST_DEV, TILE), F32)
            landing_next[slot] = jnp.zeros((3, GHOST_DEV, TILE), F32)
            landed[slot] = jnp.zeros((3, 8, TILE), F32)

    each_slot(clear)
    landing[13] = jnp.zeros((9, GHOST_DEV, TILE), F32)
    landing_next[13] = jnp.zeros((3, GHOST_DEV, TILE), F32)

    for group in range(GROUPS):
        places = [own[group, row] for row in range(3)]
        burg = [own[group, 3 + row] for row in range(3)]
        line = [own[group, 6 + row] for row in range(3)]
        fill_strengths(sides, group, burg, line)
        fill_places(sides, group, places)
        fill_across_strengths(across, group, burg, line)
        fill_across_places(across, group, places)
    fill_targets(across, targets, True)
    rows, columns = nx * CELL_DEV, plane * CELL_DEV
    row = lax.broadcasted_iota(jnp.int32, (rows, columns), 0)
    column = lax.broadcasted_iota(jnp.int32, (rows, columns), 1)
    peer = column >> 4
    step_x = (row >> 4) - gx
    step_y = gy * 4 + ((row >> 2) & 3) - (peer // nz * 4 + ((column >> 2) & 3))
    step_z = gz * 4 + (row & 3) - (peer % nz * 4 + (column & 3))
    distance2 = (step_x * step_x + step_y * step_y + step_z * step_z).astype(F32)
    weight = jnp.where(distance2 > 3.5, 1.0 / jnp.sqrt(jnp.maximum(distance2, 1.0)), 0.0)

    def wait_plane(step, carry):
        plane_copy(step).wait()
        return carry

    lax.fori_loop(1, plane, wait_plane, 0)
    contrib[...] = jnp.dot(
        weight, gathered[...], precision=lax.Precision.HIGHEST, preferred_element_type=F32
    )

    def line_copy(step):
        there = line_peer(step)[0]
        return pltpu.make_async_remote_copy(
            src_ref=contrib.at[pl.ds(pl.multiple_of(there * CELL_DEV, CELL_DEV), CELL_DEV)],
            dst_ref=arrived.at[step],
            send_sem=line_send.at[step],
            recv_sem=line_recv.at[step],
            device_id=line_peer(step),
            device_id_type=MESH,
        )

    def start_line(step, carry):
        line_copy(step).start()
        return carry

    lax.fori_loop(1, nx, start_line, 0)
    def wait_ghost(slot):
        copy, _ = ghost_copy(26 - slot)
        _, inside = place.beside(slot)

        @pl.when(inside)
        def _():
            copy.wait_recv()

    def take_ghosts(slot, carry):
        block = [landing[slot, row] for row in range(9)]
        fill_strengths(sides, GROUPS + slot, block[3:6], block[6:9])
        fill_places(sides, GROUPS + slot, block[0:3])
        return carry

    each_slot(wait_ghost)
    lax.fori_loop(0, 27, take_ghosts, 0)
    live = count_ref[0]
    near_pass(
        0, live, target_ref, from_ref, target_row[...], group_row[...], sides, targets, pairs, near
    )
    total = contrib[pl.ds(pl.multiple_of(gx * CELL_DEV, CELL_DEV), CELL_DEV), :]

    def wait_line(step, carry):
        line_copy(step).wait()
        return carry

    lax.fori_loop(1, nx, wait_line, 0)
    for step in range(1, nx):
        total = total + arrived[step]
    full = jnp.concatenate([total, jnp.zeros((TILE - CELL_DEV, 2 * TILE), F32)], axis=0)
    table_ref[pl.ds(0, TILE), :] = full[:, :TILE].T
    table_ref[pl.ds(TILE, TILE), :] = full[:, TILE:].T
    def far_pass(group):
        return far_force(
            [offset[group, row] for row in range(3)],
            [own[group, 3 + row] for row in range(3)],
            [own[group, 6 + row] for row in range(3)],
            cell_ref[pl.ds(8 * group, 8), :],
            table_ref,
        )

    for group in range(GROUPS):
        coupling = far_pass(group)
        for row in range(3):
            total = FAR_SCALE * coupling[row] + NEAR_SCALE * near[pl.ds(32 * row + 8 * group, 8), :]
            moved = offset[group, row] + STEP_SIZE * total
            force[group, row] = total
            offset[group, row] = moved
            own[group, row] = base[group, row] + moved
    for ghost in range(GHOST_DEV):
        tile = ghost_ref[ghost]
        for row in range(3):
            payload_next[row, pl.ds(ghost, 1), :] = own[tile // 8, row, pl.ds(lax.rem(tile, 8), 1), :]
    start_next, wait_next, wait_next_sent = exchange(
        place, lambda slot: payload_next, lambda slot: landing_next.at[slot], next_send, next_recv
    )
    each_slot(start_next)

    for group in range(GROUPS):
        coupling = far_pass(group)
        for row in range(3):
            far[group, row] = coupling[row]
        places = [own[group, row] for row in range(3)]
        fill_places(sides, group, places)
        fill_across_places(across, group, places)
    fill_targets(across, targets, False)
    low_ids = lax.broadcasted_iota(jnp.int32, (256, WIDTH), 0)

    def fill_lowers(block, carry):
        lanes = pl.ds(pl.multiple_of(block * WIDTH, WIDTH), WIDTH)
        for end in range(2):
            lower = dest_ref[pl.ds(end, 1), lanes] & 255
            lowers[block, :, pl.ds(end * WIDTH, WIDTH)] = jnp.where(
                low_ids == lower, 1.0, 0.0
            ).astype(BF16)
        return carry

    lax.fori_loop(0, SEG // WIDTH, fill_lowers, 0)

    def take_next(slot, carry):
        fill_places(sides, GROUPS + slot, [landing_next[slot, row] for row in range(3)])
        return carry

    each_slot(wait_next)
    lax.fori_loop(0, 27, take_next, 0)
    near_pass(
        1, live, target_ref, from_ref, target_row[...], group_row[...], sides, targets, pairs, near
    )
    for group in range(GROUPS):
        for row in range(3):
            total = FAR_SCALE * far[group, row] + NEAR_SCALE * near[pl.ds(32 * row + 8 * group, 8), :]
            moved = offset[group, row] + STEP_SIZE * total
            half = 0.5 * (force[group, row] + total)
            for tile in range(8):
                lanes = pl.ds((8 * group + tile) * TILE, TILE)
                moved_ref[pl.ds(row, 1), lanes] = moved[tile : tile + 1]
                values[pl.ds(row, 1), lanes] = half[tile : tile + 1]

    def scatter(first, count, totals):
        totals[...] = jnp.zeros(totals.shape, F32)
        high_ids = lax.broadcasted_iota(jnp.int32, (count, WIDTH), 0) + first

        def add(block, carry):
            lanes = pl.ds(pl.multiple_of(block * WIDTH, WIDTH), WIDTH)
            parts = [halves_of(values[pl.ds(row, 1), lanes]) for row in range(3)]
            lefts = []
            for end in range(2):
                dest = dest_ref[pl.ds(end, 1), lanes]
                slot = dest >> 12
                upper = jnp.where(slot == 13, 0, 16 + 4 * slot) + ((dest & (SEG - 1)) >> 8)
                chosen = high_ids == upper
                lefts.append(
                    [
                        jnp.where(chosen, parts[row][piece], 0.0).astype(BF16)
                        for row in range(3)
                        for piece in range(2)
                    ]
                )
            left = jnp.concatenate(
                [jnp.concatenate(both, axis=1) for both in zip(*lefts)], axis=0
            )
            totals[...] += lax.dot_general(left, lowers[block], NT, preferred_element_type=F32)
            return carry

        lax.fori_loop(0, SEG // WIDTH, add, 0)

    scatter(16, 112, sums)
    for row in range(3):
        for slot in range(27):
            at = 224 * row + 4 * slot
            both = sums[pl.ds(at, 4), :] + sums[pl.ds(at + 112, 4), :]
            leaving[slot, row, pl.ds(0, 4), :] = both[:, :TILE]
            leaving[slot, row, pl.ds(4, 4), :] = both[:, TILE:]
    start_node, wait_node, wait_node_sent = exchange(
        place, lambda slot: leaving.at[slot], lambda slot: landed.at[slot], node_send, node_recv
    )
    each_slot(start_node)
    scatter(0, 16, centre)
    middle = [
        centre[pl.ds(32 * row, 16), :] + centre[pl.ds(32 * row + 16, 16), :] for row in range(3)
    ]
    for row in range(3):
        for part in range(4, 16):
            nodes_ref[pl.ds(row, 1), pl.ds(256 * part, 256)] = middle[row][part : part + 1]
    each_slot(wait_node)
    for row in range(3):
        total = landed[0, row]
        for slot in range(1, 27):
            if slot != 13:
                total = total + landed[slot, row]
        for part in range(4):
            for half in range(2):
                lanes = slice(TILE * half, TILE * half + TILE)
                nodes_ref[pl.ds(row, 1), pl.ds(256 * part + TILE * half, TILE)] = (
                    middle[row][part : part + 1, lanes]
                    + total[4 * half + part : 4 * half + part + 1]
                )

    def wait_ghost_send(slot):
        copy, inside = ghost_copy(slot)

        @pl.when(inside)
        def _():
            copy.wait_send()

    each_slot(wait_ghost_send)
    each_slot(wait_next_sent)
    each_slot(wait_node_sent)


def on_device(
    sizes,
    seg_rel,
    burgers,
    line_vec,
    seg_cell,
    ghost_tiles,
    ghost_count,
    pair_target,
    pair_source,
    pair_group,
    pair_count,
    node_dest,
):
    nx, ny, nz = sizes
    plane = ny * nz
    cell = seg_cell.reshape(SEG // TILE, TILE)
    shape = jax.ShapeDtypeStruct
    dma = pltpu.SemaphoreType.DMA
    block = (GROUPS, 3, 8, TILE)
    buffers = [
        (3, SEG),
        (3, SEG),
        (3, SEG),
        (SEG // TILE, TILE, jnp.int32),
        (2, SEG, jnp.int32),
        (1, PAIRS, jnp.int32),
        (1, PAIRS, jnp.int32),
        (GROUPS, 9, 8, TILE),
        block,
        block,
        block,
        block,
        (9, GHOST_DEV, TILE),
        (27, 9, GHOST_DEV, TILE),
        (3, GHOST_DEV, TILE),
        (27, 3, GHOST_DEV, TILE),
        (40 * 32, TILE),
        (COMP * 32, TILE),
        (plane * CELL_DEV, 2 * TILE),
        (nx * CELL_DEV, 2 * TILE),
        (nx, CELL_DEV, 2 * TILE),
        (2 * TILE, TILE),
        ((GROUPS + 27) * SIDE, TILE),
        (GROUPS * ACROSS, TILE),
        (SEG // TILE, 48, 4 * TILE, BF16),
        (3 * PAIRS, TILE),
        (3 * SEG // TILE, TILE),
        (8, SEG),
        (SEG // WIDTH, 256, 2 * WIDTH, BF16),
        (96, 256),
        (672, 256),
        (27, 3, 8, TILE),
        (27, 3, 8, TILE),
    ]
    scratch = []
    for sides in buffers:
        kind = F32
        if not isinstance(sides[-1], int):
            sides, kind = sides[:-1], sides[-1]
        scratch.append(pltpu.VMEM(sides, kind))
    return pl.pallas_call(
        functools.partial(step_kernel, sizes),
        out_shape=(shape((3, SEG), F32), shape((3, SEG), F32)),
        in_specs=smem(5) + [pl.BlockSpec(memory_space=pl.ANY)] * 7,
        out_specs=tuple(vmem(2)),
        scratch_shapes=scratch
        + [dma((7,))]
        + [dma((27,))] * 6
        + [dma((plane,))] * 2
        + [dma((nx,))] * 2,
        compiler_params=pltpu.CompilerParams(
            collective_id=0, has_side_effects=True, vmem_limit_bytes=56 << 20
        ),
        name="step",
    )(
        ghost_tiles,
        ghost_count,
        pair_count,
        pair_target,
        pair_source,
        seg_rel,
        burgers,
        line_vec,
        cell,
        node_dest,
        pair_target.reshape(1, PAIRS),
        pair_group.reshape(1, PAIRS),
    )


def solution(mesh):
    sizes = tuple(mesh.shape[name] for name in ("gx", "gy", "gz"))
    whole = ("gx", "gy", "gz")
    return jax.shard_map(
        functools.partial(on_device, sizes),
        mesh=mesh,
        in_specs=(P(None, whole),) * 3 + (P(whole),) * 7 + (P(None, whole),),
        out_specs=(P(None, whole), P(None, whole)),
        check_vma=False,
    )
```

```python
import functools

import jax
import jax.numpy as jnp
from jax import lax
from jax.experimental import pallas as pl
from jax.experimental.pallas import tpu as pltpu
from jax.sharding import PartitionSpec as P

TILE = 128
SEG = 4096
GROUPS = 4
GHOST_DEV = 8
CELL_DEV = 16
COMP = 6
TERMS = 35
LANE_STEP = 42
PAIRS = 128
CORE2 = 0.25
NEAR_SCALE = 0.05
FAR_SCALE = 0.002
STEP_SIZE = 0.1
MESH = pl.DeviceIdType.MESH
F32 = jnp.float32
BF16 = jnp.bfloat16
EXPONENTS = [
    (a, b, degree - a - b)
    for degree in range(5)
    for a in range(degree, -1, -1)
    for b in range(degree - a, -1, -1)
]
NT = (((1,), (1,)), ((), ()))
TN = (((0,), (0,)), ((), ()))


def vmem(count):
    return [pl.BlockSpec(memory_space=pltpu.VMEM)] * count


def smem(count):
    return [pl.BlockSpec(memory_space=pltpu.SMEM)] * count


def halves_of(value):
    high = value.astype(BF16).astype(F32)
    return high, value - high


def powers(unit):
    square = unit * unit
    return [None, unit, square, square * unit, square * square]


def monomial(u, v, w, exps):
    result = None
    for table, power in zip((u, v, w), exps):
        if power:
            result = table[power] if result is None else result * table[power]
    return result


def symmetric(b, t):
    return [
        b[0] * t[0],
        b[1] * t[1],
        b[2] * t[2],
        0.5 * (b[0] * t[1] + b[1] * t[0]),
        0.5 * (b[1] * t[2] + b[2] * t[1]),
        0.5 * (b[0] * t[2] + b[2] * t[0]),
    ]


class Place:
    def __init__(self, sizes):
        self.sizes = sizes
        self.at = tuple(lax.axis_index(name) for name in ("gx", "gy", "gz"))
        self.free = [
            {-1: at > 0, 1: at < size - 1} for at, size in zip(self.at, sizes)
        ]

    def beside(self, slot):
        steps = (slot // 9 - 1, slot // 3 % 3 - 1, slot % 3 - 1)
        where = tuple(at + step for at, step in zip(self.at, steps))
        inside = None
        for free, step in zip(self.free, steps):
            if step:
                inside = free[step] if inside is None else jnp.logical_and(inside, free[step])
        return where, inside

    def count_beside(self):
        total = 1
        for at, size in zip(self.at, self.sizes):
            total = total * (3 - (at == 0).astype(jnp.int32) - (at == size - 1).astype(jnp.int32))
        return total - 1


def each_slot(body):
    for slot in range(27):
        if slot != 13:
            body(slot)


def greet_neighbours(place, barrier):
    def greet(slot):
        where, inside = place.beside(slot)

        @pl.when(inside)
        def _():
            pl.semaphore_signal(barrier, inc=1, device_id=where, device_id_type=MESH)

    each_slot(greet)


def far_force(offset, burg, line, cell, table_ref):
    u, v, w = (powers(2.0 * value) for value in offset)
    stress = [None] * COMP
    for at, exps in enumerate(EXPONENTS):
        value = monomial(u, v, w, exps)
        for comp in range(COMP):
            row = comp // 3 * TILE + comp % 3 * LANE_STEP + at
            entry = jnp.broadcast_to(table_ref[pl.ds(row, 1), :], (8, TILE))
            term = jnp.take_along_axis(entry, cell, axis=1, mode="promise_in_bounds")
            if value is not None:
                term = term * value
            stress[comp] = term if stress[comp] is None else stress[comp] + term
    push_x = stress[0] * burg[0] + stress[3] * burg[1] + stress[5] * burg[2]
    push_y = stress[3] * burg[0] + stress[1] * burg[1] + stress[4] * burg[2]
    push_z = stress[5] * burg[0] + stress[4] * burg[1] + stress[2] * burg[2]
    return [
        push_y * line[2] - push_z * line[1],
        push_z * line[0] - push_x * line[2],
        push_x * line[1] - push_y * line[0],
    ]


def exchange(place, send_of, receive_at, send_sem, recv_sem):
    def copy_of(slot):
        where, inside = place.beside(slot)
        copy = pltpu.make_async_remote_copy(
            src_ref=send_of(slot),
            dst_ref=receive_at(26 - slot),
            send_sem=send_sem.at[slot],
            recv_sem=recv_sem.at[26 - slot],
            device_id=where,
            device_id_type=MESH,
        )
        return copy, inside

    def start(slot):
        copy, inside = copy_of(slot)

        @pl.when(inside)
        def _():
            copy.start()

    def wait(slot):
        arriving, _ = copy_of(26 - slot)
        _, inside = place.beside(slot)

        @pl.when(inside)
        def _():
            arriving.wait_recv()

    def wait_sent(slot):
        copy, inside = copy_of(slot)

        @pl.when(inside)
        def _():
            copy.wait_send()

    return start, wait, wait_sent


SIDE = 48 * 8
ACROSS = 80 * 8
UNROLL = 32
WIDTH = 512


def pieces_of(value):
    high = value.astype(BF16).astype(F32)
    rest = value - high
    middle = rest.astype(BF16).astype(F32)
    return [high, middle, rest - middle]


def product_halves(burg, line):
    highs, lows = [], []
    for b in burg:
        for t in line:
            high, low = halves_of(b * t)
            highs.append(high)
            lows.append(low)
    return highs, lows


def store_rows(ref, at, rows):
    for row, value in enumerate(rows):
        ref[pl.ds(at + 8 * row, 8), :] = value


def fill_strengths(sides, group, burg, line):
    highs, lows = product_halves(burg, line)
    zero, one = jnp.zeros((8, TILE), F32), jnp.ones((8, TILE), F32)
    at = pl.multiple_of(group * SIDE, SIDE)
    store_rows(sides, at, highs + highs + lows + [zero] * 5)
    store_rows(sides, at + 41 * 8, [one] * 3 + [zero] * 4)


def fill_places(sides, group, places):
    at = pl.multiple_of(group * SIDE, SIDE)
    store_rows(sides, at + 32 * 8, [piece for place in places for piece in pieces_of(place)])


def fill_across_strengths(across, group, burg, line):
    highs, lows = product_halves(burg, line)
    zero = jnp.zeros((8, TILE), F32)
    store_rows(across, group * ACROSS, highs + lows + highs + [zero] * 5)


def fill_across_places(across, group, places):
    zero, one = jnp.zeros((8, TILE), F32), jnp.ones((8, TILE), F32)
    for row in range(3):
        signs = [-one if at // 3 == row else zero for at in range(9)]
        store_rows(
            across,
            group * ACROSS + (32 + 16 * row) * 8,
            signs + pieces_of(places[row]) + [zero] * 4,
        )


def fill_targets(across, targets, strengths):
    def fill(tile, carry):
        at = tile // 8 * ACROSS + tile % 8
        if strengths:
            top = across[pl.ds(at, 32, stride=8), :]
            zero = jnp.zeros((32, 3 * TILE), F32)
            targets[tile, pl.ds(0, 32), :] = jnp.concatenate([top, zero], axis=1).astype(BF16)
        low = [across[pl.ds(at + (32 + 16 * row) * 8, 16, stride=8), :] for row in range(3)]
        low = jnp.concatenate([jnp.zeros((16, TILE), F32)] + low, axis=1)
        targets[tile, pl.ds(32, 16), :] = low.astype(BF16)
        return carry

    lax.fori_loop(0, SEG // TILE, fill, 0)


def near_pass(sweep, live, target_ref, from_ref, target_row, group_row, sides, targets, pairs, near):
    def forces_of_pair(pair):
        source = from_ref[pair]
        left = sides[pl.ds((source >> 3) * SIDE + (source & 7), 48, stride=8), :]
        both = lax.dot_general(
            left.astype(BF16), targets[target_ref[pair]], TN, preferred_element_type=F32
        )
        totals = [jnp.zeros((8, TILE), F32)] * 3
        for chunk in range(16):
            span = both[8 * chunk : 8 * chunk + 8]
            gaps = [span[:, TILE * (row + 1) : TILE * (row + 2)] for row in range(3)]
            radius2 = gaps[0] * gaps[0] + gaps[1] * gaps[1] + gaps[2] * gaps[2] + CORE2
            inverse = lax.rsqrt(radius2)
            weight = span[:, :TILE] * (inverse * inverse * inverse)
            totals = [total + weight * gap for total, gap in zip(totals, gaps)]
        return totals

    def step(block, carry):
        results = [forces_of_pair(block * UNROLL + at) for at in range(UNROLL)]
        for row in range(3):
            rows = [jnp.sum(totals[row], axis=0, keepdims=True) for totals in results]
            at = pl.multiple_of(row * PAIRS + block * UNROLL, UNROLL)
            pairs[pl.ds(at, UNROLL), :] = jnp.concatenate(rows, axis=0)
        return carry

    lax.fori_loop(0, PAIRS // UNROLL, step, 0)
    tile_ids = lax.broadcasted_iota(jnp.int32, (SEG // TILE, PAIRS), 0)
    pair_ids = lax.broadcasted_iota(jnp.int32, (SEG // TILE, PAIRS), 1)
    wanted = (tile_ids == target_row) & (group_row == sweep) & (pair_ids < live)
    select = jnp.where(wanted, 1.0, 0.0).astype(BF16)
    for row in range(3):
        total = None
        for piece in pieces_of(pairs[pl.ds(row * PAIRS, PAIRS), :]):
            part = jnp.dot(select, piece.astype(BF16), preferred_element_type=F32)
            total = part if total is None else total + part
        near[pl.ds(32 * row, 32), :] = total


def step_kernel(
    sizes,
    ghost_hbm,
    live_hbm,
    count_hbm,
    target_scalars,
    from_hbm,
    rel_hbm,
    burg_hbm,
    line_hbm,
    cell_hbm,
    dest_hbm,
    target_hbm,
    group_hbm,
    moved_hbm,
    nodes_hbm,
    ghost_ref,
    live_ref,
    count_ref,
    target_ref,
    from_ref,
    moved_ref,
    nodes_ref,
    rel_ref,
    burg_ref,
    line_ref,
    cell_ref,
    dest_ref,
    target_row,
    group_row,
    own,
    base,
    offset,
    force,
    far,
    payload,
    landing,
    payload_next,
    landing_next,
    mono,
    symm,
    gathered,
    contrib,
    arrived,
    table_ref,
    sides,
    across,
    targets,
    pairs,
    near,
    values,
    lowers,
    centre,
    sums,
    leaving,
    landed,
    load_sem,
    out_sem,
    ghost_send,
    ghost_recv,
    next_send,
    next_recv,
    node_send,
    node_recv,
    plane_send,
    plane_recv,
    line_send,
    line_recv,
):
    loads = [
        pltpu.make_async_copy(source, target, load_sem.at[at])
        for at, (source, target) in enumerate(
            [
                (ghost_hbm, ghost_ref),
                (live_hbm, live_ref),
                (count_hbm, count_ref),
                (target_scalars, target_ref),
                (from_hbm, from_ref),
                (rel_hbm, rel_ref),
                (burg_hbm, burg_ref),
                (line_hbm, line_ref),
                (cell_hbm, cell_ref),
                (dest_hbm, dest_ref),
                (target_hbm, target_row),
                (group_hbm, group_row),
            ]
        )
    ]
    for load in loads:
        load.start()
    nx, ny, nz = sizes
    plane = ny * nz
    place = Place(sizes)
    gx, gy, gz = place.at
    here = gy * nz + gz

    def plane_peer(step):
        peer = here + step
        peer = jnp.where(peer >= plane, peer - plane, peer)
        row = sum((peer >= nz * at).astype(jnp.int32) for at in range(1, ny))
        return (gx, row, peer - nz * row)

    def line_peer(step):
        there = gx + step
        return (jnp.where(there >= nx, there - nx, there), gy, gz)

    barrier = pltpu.get_barrier_semaphore()
    greet_neighbours(place, barrier)

    def greet_plane(step, carry):
        pl.semaphore_signal(barrier, inc=1, device_id=plane_peer(step), device_id_type=MESH)
        return carry

    def greet_line(step, carry):
        pl.semaphore_signal(barrier, inc=1, device_id=line_peer(step), device_id_type=MESH)
        return carry

    lax.fori_loop(1, plane, greet_plane, 0)
    lax.fori_loop(1, nx, greet_line, 0)

    for load in loads:
        load.wait()
    for tile in range(SEG // TILE):
        lanes = pl.ds(tile * TILE, TILE)
        for row in range(3):
            own[tile // 8, row, pl.ds(tile % 8, 1), :] = rel_ref[pl.ds(row, 1), lanes]
            own[tile // 8, 3 + row, pl.ds(tile % 8, 1), :] = burg_ref[pl.ds(row, 1), lanes]
            own[tile // 8, 6 + row, pl.ds(tile % 8, 1), :] = line_ref[pl.ds(row, 1), lanes]
    for group in range(GROUPS):
        rows = slice(8 * group, 8 * group + 8)
        cell = cell_ref[rows, :]
        rel = [own[group, row] for row in range(3)]
        burg = [own[group, 3 + row] for row in range(3)]
        line = [own[group, 6 + row] for row in range(3)]
        corner = (
            jnp.full((8, TILE), gx, jnp.int32),
            gy * 4 + (cell >> 2),
            gz * 4 + (cell & 3),
        )
        for row in range(3):
            corner_row = corner[row].astype(F32) + 0.5
            base[group, row] = corner_row
            offset[group, row] = rel[row]
            own[group, row] = corner_row + rel[row]
        for at, value in enumerate(symmetric(burg, line)):
            symm[pl.ds(at * 32 + 8 * group, 8), :] = value
        u, v, w = (powers(2.0 * value) for value in rel)
        for at, exps in enumerate(EXPONENTS):
            value = monomial(u, v, w, exps)
            mono[pl.ds(at * 32 + 8 * group, 8), :] = (
                jnp.ones((8, TILE), F32) if value is None else value
            )
    for at in range(TERMS, 40):
        mono[pl.ds(at * 32, 32), :] = jnp.zeros((32, TILE), F32)
    for ghost in range(GHOST_DEV):
        tile = ghost_ref[ghost]
        live = jnp.where(ghost < live_ref[0], 1.0, 0.0)
        for row in range(9):
            value = own[tile // 8, row, pl.ds(lax.rem(tile, 8), 1), :]
            payload[row, pl.ds(ghost, 1), :] = value * live

    cells = lax.broadcasted_iota(jnp.int32, (CELL_DEV, TILE), 0)
    moments = jnp.zeros((COMP * CELL_DEV, 40), F32)
    for block in range(4):
        lefts, rights = [], []
        for tile in range(8 * block, 8 * block + 8):
            chosen = cells == cell_ref[pl.ds(tile, 1), :]
            left = jnp.concatenate(
                [
                    jnp.where(chosen, symm[pl.ds(at * 32 + tile, 1), :], 0.0)
                    for at in range(COMP)
                ],
                axis=0,
            )
            right = mono[pl.ds(tile, 40, stride=32), :]
            left_high, left_low = halves_of(left)
            right_high, right_low = halves_of(right)
            lefts += [left_high, left_high, left_low]
            rights += [right_high, right_low, right_high]
        moments = moments + lax.dot_general(
            jnp.concatenate(lefts, axis=1).astype(BF16),
            jnp.concatenate(rights, axis=1).astype(BF16),
            NT,
            preferred_element_type=F32,
        )
    wide = jnp.concatenate([moments, jnp.zeros((COMP * CELL_DEV, TILE - 40), F32)], axis=1)
    mine = pl.ds(pl.multiple_of(here * CELL_DEV, CELL_DEV), CELL_DEV)
    for half in range(2):
        total = jnp.zeros((CELL_DEV, TILE), F32)
        for third in range(3):
            at = (3 * half + third) * CELL_DEV
            part = wide[at : at + CELL_DEV]
            total = total + (pltpu.roll(part, third * LANE_STEP, 1) if third else part)
        gathered[mine, pl.ds(half * TILE, TILE)] = total

    pl.semaphore_wait(barrier, place.count_beside() + plane - 1 + nx - 1)

    def plane_copy(step):
        return pltpu.make_async_remote_copy(
            src_ref=gathered.at[mine],
            dst_ref=gathered.at[mine],
            send_sem=plane_send.at[step],
            recv_sem=plane_recv.at[step],
            device_id=plane_peer(step),
            device_id_type=MESH,
        )

    def ghost_copy(slot):
        where, inside = place.beside(slot)
        copy = pltpu.make_async_remote_copy(
            src_ref=payload,
            dst_ref=landing.at[26 - slot],
            send_sem=ghost_send.at[slot],
            recv_sem=ghost_recv.at[26 - slot],
            device_id=where,
            device_id_type=MESH,
        )
        return copy, inside

    def start_plane(step, carry):
        plane_copy(step).start()
        return carry

    lax.fori_loop(1, plane, start_plane, 0)

    def start_ghost(slot):
        copy, inside = ghost_copy(slot)

        @pl.when(inside)
        def _():
            copy.start()

    each_slot(start_ghost)

    def clear(slot):
        _, inside = place.beside(slot)

        @pl.when(jnp.logical_not(inside))
        def _():
            landing[slot] = jnp.zeros((9, GHOST_DEV, TILE), F32)
            landing_next[slot] = jnp.zeros((3, GHOST_DEV, TILE), F32)
            landed[slot] = jnp.zeros((3, 8, TILE), F32)

    each_slot(clear)
    landing[13] = jnp.zeros((9, GHOST_DEV, TILE), F32)
    landing_next[13] = jnp.zeros((3, GHOST_DEV, TILE), F32)

    for group in range(GROUPS):
        places = [own[group, row] for row in range(3)]
        burg = [own[group, 3 + row] for row in range(3)]
        line = [own[group, 6 + row] for row in range(3)]
        fill_strengths(sides, group, burg, line)
        fill_places(sides, group, places)
        fill_across_strengths(across, group, burg, line)
        fill_across_places(across, group, places)
    fill_targets(across, targets, True)
    rows, columns = nx * CELL_DEV, plane * CELL_DEV
    row = lax.broadcasted_iota(jnp.int32, (rows, columns), 0)
    column = lax.broadcasted_iota(jnp.int32, (rows, columns), 1)
    peer = column >> 4
    step_x = (row >> 4) - gx
    step_y = gy * 4 + ((row >> 2) & 3) - (peer // nz * 4 + ((column >> 2) & 3))
    step_z = gz * 4 + (row & 3) - (peer % nz * 4 + (column & 3))
    distance2 = (step_x * step_x + step_y * step_y + step_z * step_z).astype(F32)
    weight = jnp.where(distance2 > 3.5, 1.0 / jnp.sqrt(jnp.maximum(distance2, 1.0)), 0.0)

    def wait_plane(step, carry):
        plane_copy(step).wait()
        return carry

    lax.fori_loop(1, plane, wait_plane, 0)
    contrib[...] = jnp.dot(
        weight, gathered[...], precision=lax.Precision.HIGHEST, preferred_element_type=F32
    )

    def line_copy(step):
        there = line_peer(step)[0]
        return pltpu.make_async_remote_copy(
            src_ref=contrib.at[pl.ds(pl.multiple_of(there * CELL_DEV, CELL_DEV), CELL_DEV)],
            dst_ref=arrived.at[step],
            send_sem=line_send.at[step],
            recv_sem=line_recv.at[step],
            device_id=line_peer(step),
            device_id_type=MESH,
        )

    def start_line(step, carry):
        line_copy(step).start()
        return carry

    lax.fori_loop(1, nx, start_line, 0)
    def wait_ghost(slot):
        copy, _ = ghost_copy(26 - slot)
        _, inside = place.beside(slot)

        @pl.when(inside)
        def _():
            copy.wait_recv()

    def take_ghosts(slot, carry):
        block = [landing[slot, row] for row in range(9)]
        fill_strengths(sides, GROUPS + slot, block[3:6], block[6:9])
        fill_places(sides, GROUPS + slot, block[0:3])
        return carry

    each_slot(wait_ghost)
    lax.fori_loop(0, 27, take_ghosts, 0)
    live = count_ref[0]
    near_pass(
        0, live, target_ref, from_ref, target_row[...], group_row[...], sides, targets, pairs, near
    )
    total = contrib[pl.ds(pl.multiple_of(gx * CELL_DEV, CELL_DEV), CELL_DEV), :]

    def wait_line(step, carry):
        line_copy(step).wait()
        return carry

    lax.fori_loop(1, nx, wait_line, 0)
    for step in range(1, nx):
        total = total + arrived[step]
    full = jnp.concatenate([total, jnp.zeros((TILE - CELL_DEV, 2 * TILE), F32)], axis=0)
    table_ref[pl.ds(0, TILE), :] = full[:, :TILE].T
    table_ref[pl.ds(TILE, TILE), :] = full[:, TILE:].T
    def far_pass(group):
        return far_force(
            [offset[group, row] for row in range(3)],
            [own[group, 3 + row] for row in range(3)],
            [own[group, 6 + row] for row in range(3)],
            cell_ref[pl.ds(8 * group, 8), :],
            table_ref,
        )

    for group in range(GROUPS):
        coupling = far_pass(group)
        for row in range(3):
            total = FAR_SCALE * coupling[row] + NEAR_SCALE * near[pl.ds(32 * row + 8 * group, 8), :]
            moved = offset[group, row] + STEP_SIZE * total
            force[group, row] = total
            offset[group, row] = moved
            own[group, row] = base[group, row] + moved
    for ghost in range(GHOST_DEV):
        tile = ghost_ref[ghost]
        for row in range(3):
            payload_next[row, pl.ds(ghost, 1), :] = own[tile // 8, row, pl.ds(lax.rem(tile, 8), 1), :]
    start_next, wait_next, wait_next_sent = exchange(
        place, lambda slot: payload_next, lambda slot: landing_next.at[slot], next_send, next_recv
    )
    each_slot(start_next)

    for group in range(GROUPS):
        coupling = far_pass(group)
        for row in range(3):
            far[group, row] = coupling[row]
        places = [own[group, row] for row in range(3)]
        fill_places(sides, group, places)
        fill_across_places(across, group, places)
    fill_targets(across, targets, False)
    low_ids = lax.broadcasted_iota(jnp.int32, (256, WIDTH), 0)

    def fill_lowers(block, carry):
        lanes = pl.ds(pl.multiple_of(block * WIDTH, WIDTH), WIDTH)
        for end in range(2):
            lower = dest_ref[pl.ds(end, 1), lanes] & 255
            lowers[block, :, pl.ds(end * WIDTH, WIDTH)] = jnp.where(
                low_ids == lower, 1.0, 0.0
            ).astype(BF16)
        return carry

    lax.fori_loop(0, SEG // WIDTH, fill_lowers, 0)

    def take_next(slot, carry):
        fill_places(sides, GROUPS + slot, [landing_next[slot, row] for row in range(3)])
        return carry

    each_slot(wait_next)
    lax.fori_loop(0, 27, take_next, 0)
    near_pass(
        1, live, target_ref, from_ref, target_row[...], group_row[...], sides, targets, pairs, near
    )
    for group in range(GROUPS):
        for row in range(3):
            total = FAR_SCALE * far[group, row] + NEAR_SCALE * near[pl.ds(32 * row + 8 * group, 8), :]
            moved = offset[group, row] + STEP_SIZE * total
            half = 0.5 * (force[group, row] + total)
            for tile in range(8):
                lanes = pl.ds((8 * group + tile) * TILE, TILE)
                moved_ref[pl.ds(row, 1), lanes] = moved[tile : tile + 1]
                values[pl.ds(row, 1), lanes] = half[tile : tile + 1]

    save_moved = pltpu.make_async_copy(moved_ref, moved_hbm, out_sem.at[0])
    save_moved.start()

    def scatter(first, count, totals):
        totals[...] = jnp.zeros(totals.shape, F32)
        high_ids = lax.broadcasted_iota(jnp.int32, (count, WIDTH), 0) + first

        def add(block, carry):
            lanes = pl.ds(pl.multiple_of(block * WIDTH, WIDTH), WIDTH)
            parts = [halves_of(values[pl.ds(row, 1), lanes]) for row in range(3)]
            lefts = []
            for end in range(2):
                dest = dest_ref[pl.ds(end, 1), lanes]
                slot = dest >> 12
                upper = jnp.where(slot == 13, 0, 16 + 4 * slot) + ((dest & (SEG - 1)) >> 8)
                chosen = high_ids == upper
                lefts.append(
                    [
                        jnp.where(chosen, parts[row][piece], 0.0).astype(BF16)
                        for row in range(3)
                        for piece in range(2)
                    ]
                )
            left = jnp.concatenate(
                [jnp.concatenate(both, axis=1) for both in zip(*lefts)], axis=0
            )
            totals[...] += lax.dot_general(left, lowers[block], NT, preferred_element_type=F32)
            return carry

        lax.fori_loop(0, SEG // WIDTH, add, 0)

    scatter(16, 112, sums)
    for row in range(3):
        for slot in range(27):
            at = 224 * row + 4 * slot
            both = sums[pl.ds(at, 4), :] + sums[pl.ds(at + 112, 4), :]
            leaving[slot, row, pl.ds(0, 4), :] = both[:, :TILE]
            leaving[slot, row, pl.ds(4, 4), :] = both[:, TILE:]
    start_node, wait_node, wait_node_sent = exchange(
        place, lambda slot: leaving.at[slot], lambda slot: landed.at[slot], node_send, node_recv
    )
    each_slot(start_node)
    scatter(0, 16, centre)
    middle = [
        centre[pl.ds(32 * row, 16), :] + centre[pl.ds(32 * row + 16, 16), :] for row in range(3)
    ]
    for row in range(3):
        for part in range(4, 16):
            nodes_ref[pl.ds(row, 1), pl.ds(256 * part, 256)] = middle[row][part : part + 1]
    inner = pl.ds(1024, SEG - 1024)
    save_inner = pltpu.make_async_copy(
        nodes_ref.at[:, inner], nodes_hbm.at[:, inner], out_sem.at[1]
    )
    save_inner.start()
    each_slot(wait_node)
    for row in range(3):
        total = landed[0, row]
        for slot in range(1, 27):
            if slot != 13:
                total = total + landed[slot, row]
        for part in range(4):
            for half in range(2):
                lanes = slice(TILE * half, TILE * half + TILE)
                nodes_ref[pl.ds(row, 1), pl.ds(256 * part + TILE * half, TILE)] = (
                    middle[row][part : part + 1, lanes]
                    + total[4 * half + part : 4 * half + part + 1]
                )

    outer = pl.ds(0, 1024)
    save_outer = pltpu.make_async_copy(
        nodes_ref.at[:, outer], nodes_hbm.at[:, outer], out_sem.at[2]
    )
    save_outer.start()

    def wait_ghost_send(slot):
        copy, inside = ghost_copy(slot)

        @pl.when(inside)
        def _():
            copy.wait_send()

    each_slot(wait_ghost_send)
    each_slot(wait_next_sent)
    each_slot(wait_node_sent)
    for save in (save_moved, save_inner, save_outer):
        save.wait()


def on_device(
    sizes,
    seg_rel,
    burgers,
    line_vec,
    seg_cell,
    ghost_tiles,
    ghost_count,
    pair_target,
    pair_source,
    pair_group,
    pair_count,
    node_dest,
):
    nx, ny, nz = sizes
    plane = ny * nz
    cell = seg_cell.reshape(SEG // TILE, TILE)
    shape = jax.ShapeDtypeStruct
    dma = pltpu.SemaphoreType.DMA
    block = (GROUPS, 3, 8, TILE)
    buffers = [
        (3, SEG),
        (3, SEG),
        (3, SEG),
        (3, SEG),
        (3, SEG),
        (SEG // TILE, TILE, jnp.int32),
        (2, SEG, jnp.int32),
        (1, PAIRS, jnp.int32),
        (1, PAIRS, jnp.int32),
        (GROUPS, 9, 8, TILE),
        block,
        block,
        block,
        block,
        (9, GHOST_DEV, TILE),
        (27, 9, GHOST_DEV, TILE),
        (3, GHOST_DEV, TILE),
        (27, 3, GHOST_DEV, TILE),
        (40 * 32, TILE),
        (COMP * 32, TILE),
        (plane * CELL_DEV, 2 * TILE),
        (nx * CELL_DEV, 2 * TILE),
        (nx, CELL_DEV, 2 * TILE),
        (2 * TILE, TILE),
        ((GROUPS + 27) * SIDE, TILE),
        (GROUPS * ACROSS, TILE),
        (SEG // TILE, 48, 4 * TILE, BF16),
        (3 * PAIRS, TILE),
        (3 * SEG // TILE, TILE),
        (8, SEG),
        (SEG // WIDTH, 256, 2 * WIDTH, BF16),
        (96, 256),
        (672, 256),
        (27, 3, 8, TILE),
        (27, 3, 8, TILE),
    ]
    scratch = []
    for sides in buffers:
        kind = F32
        if not isinstance(sides[-1], int):
            sides, kind = sides[:-1], sides[-1]
        scratch.append(pltpu.VMEM(sides, kind))
    return pl.pallas_call(
        functools.partial(step_kernel, sizes),
        out_shape=(shape((3, SEG), F32), shape((3, SEG), F32)),
        in_specs=[pl.BlockSpec(memory_space=pl.ANY)] * 12,
        out_specs=(pl.BlockSpec(memory_space=pl.ANY),) * 2,
        scratch_shapes=[
            pltpu.SMEM((count,), jnp.int32) for count in (GHOST_DEV, 1, 1, PAIRS, PAIRS)
        ]
        + scratch
        + [dma((12,)), dma((3,))]
        + [dma((27,))] * 6
        + [dma((plane,))] * 2
        + [dma((nx,))] * 2,
        compiler_params=pltpu.CompilerParams(
            collective_id=0, has_side_effects=True, vmem_limit_bytes=56 << 20
        ),
        name="step",
    )(
        ghost_tiles,
        ghost_count,
        pair_count,
        pair_target,
        pair_source,
        seg_rel,
        burgers,
        line_vec,
        cell,
        node_dest,
        pair_target.reshape(1, PAIRS),
        pair_group.reshape(1, PAIRS),
    )


def solution(mesh):
    sizes = tuple(mesh.shape[name] for name in ("gx", "gy", "gz"))
    whole = ("gx", "gy", "gz")
    return jax.shard_map(
        functools.partial(on_device, sizes),
        mesh=mesh,
        in_specs=(P(None, whole),) * 3 + (P(whole),) * 7 + (P(None, whole),),
        out_specs=(P(None, whole), P(None, whole)),
        check_vma=False,
    )
```

```python
import functools

import jax
import jax.numpy as jnp
from jax import lax
from jax.experimental import pallas as pl
from jax.experimental.pallas import tpu as pltpu
from jax.sharding import PartitionSpec as P

TILE = 128
SEG = 4096
GROUPS = 4
GHOST_DEV = 8
CELL_DEV = 16
COMP = 6
TERMS = 35
LANE_STEP = 42
PAIRS = 128
CORE2 = 0.25
NEAR_SCALE = 0.05
FAR_SCALE = 0.002
STEP_SIZE = 0.1
MESH = pl.DeviceIdType.MESH
F32 = jnp.float32
BF16 = jnp.bfloat16
EXPONENTS = [
    (a, b, degree - a - b)
    for degree in range(5)
    for a in range(degree, -1, -1)
    for b in range(degree - a, -1, -1)
]
NT = (((1,), (1,)), ((), ()))
TN = (((0,), (0,)), ((), ()))


def vmem(count):
    return [pl.BlockSpec(memory_space=pltpu.VMEM)] * count


def smem(count):
    return [pl.BlockSpec(memory_space=pltpu.SMEM)] * count


def halves_of(value):
    high = value.astype(BF16).astype(F32)
    return high, value - high


def powers(unit):
    square = unit * unit
    return [None, unit, square, square * unit, square * square]


def monomial(u, v, w, exps):
    result = None
    for table, power in zip((u, v, w), exps):
        if power:
            result = table[power] if result is None else result * table[power]
    return result


def symmetric(b, t):
    return [
        b[0] * t[0],
        b[1] * t[1],
        b[2] * t[2],
        0.5 * (b[0] * t[1] + b[1] * t[0]),
        0.5 * (b[1] * t[2] + b[2] * t[1]),
        0.5 * (b[0] * t[2] + b[2] * t[0]),
    ]


class Place:
    def __init__(self, sizes):
        self.sizes = sizes
        self.at = tuple(lax.axis_index(name) for name in ("gx", "gy", "gz"))
        self.free = [
            {-1: at > 0, 1: at < size - 1} for at, size in zip(self.at, sizes)
        ]

    def beside(self, slot):
        steps = (slot // 9 - 1, slot // 3 % 3 - 1, slot % 3 - 1)
        where = tuple(at + step for at, step in zip(self.at, steps))
        inside = None
        for free, step in zip(self.free, steps):
            if step:
                inside = free[step] if inside is None else jnp.logical_and(inside, free[step])
        return where, inside

    def inside(self, step_x, step_z):
        found = True
        for free, step in ((self.free[0], step_x), (self.free[2], step_z)):
            if step:
                found = free[step] if found is True else jnp.logical_and(found, free[step])
        return found

    def count_beside(self):
        total = 1
        for at, size in zip(self.at, self.sizes):
            total = total * (3 - (at == 0).astype(jnp.int32) - (at == size - 1).astype(jnp.int32))
        return total - 1


def each_slot(body):
    for slot in range(27):
        if slot != 13:
            body(slot)


def greet_neighbours(place, barrier):
    def greet(slot):
        where, inside = place.beside(slot)

        @pl.when(inside)
        def _():
            pl.semaphore_signal(barrier, inc=1, device_id=where, device_id_type=MESH)

    each_slot(greet)


def far_force(offset, burg, line, cell, table_ref):
    u, v, w = (powers(2.0 * value) for value in offset)
    stress = [None] * COMP
    for at, exps in enumerate(EXPONENTS):
        value = monomial(u, v, w, exps)
        for comp in range(COMP):
            row = comp // 3 * TILE + comp % 3 * LANE_STEP + at
            entry = jnp.broadcast_to(table_ref[pl.ds(row, 1), :], (8, TILE))
            term = jnp.take_along_axis(entry, cell, axis=1, mode="promise_in_bounds")
            if value is not None:
                term = term * value
            stress[comp] = term if stress[comp] is None else stress[comp] + term
    push_x = stress[0] * burg[0] + stress[3] * burg[1] + stress[5] * burg[2]
    push_y = stress[3] * burg[0] + stress[1] * burg[1] + stress[4] * burg[2]
    push_z = stress[5] * burg[0] + stress[4] * burg[1] + stress[2] * burg[2]
    return [
        push_y * line[2] - push_z * line[1],
        push_z * line[0] - push_x * line[2],
        push_x * line[1] - push_y * line[0],
    ]


def exchange(place, send_of, receive_at, send_sem, recv_sem):
    def copy_of(slot):
        where, inside = place.beside(slot)
        copy = pltpu.make_async_remote_copy(
            src_ref=send_of(slot),
            dst_ref=receive_at(26 - slot),
            send_sem=send_sem.at[slot],
            recv_sem=recv_sem.at[26 - slot],
            device_id=where,
            device_id_type=MESH,
        )
        return copy, inside

    def start(slot):
        copy, inside = copy_of(slot)

        @pl.when(inside)
        def _():
            copy.start()

    def wait(slot):
        arriving, _ = copy_of(26 - slot)
        _, inside = place.beside(slot)

        @pl.when(inside)
        def _():
            arriving.wait_recv()

    def wait_sent(slot):
        copy, inside = copy_of(slot)

        @pl.when(inside)
        def _():
            copy.wait_send()

    return start, wait, wait_sent


SIDE = 48 * 8
ACROSS = 80 * 8
UNROLL = 32
WIDTH = 512


def pieces_of(value):
    high = value.astype(BF16).astype(F32)
    rest = value - high
    middle = rest.astype(BF16).astype(F32)
    return [high, middle, rest - middle]


def product_halves(burg, line):
    highs, lows = [], []
    for b in burg:
        for t in line:
            high, low = halves_of(b * t)
            highs.append(high)
            lows.append(low)
    return highs, lows


def store_rows(ref, at, rows):
    for row, value in enumerate(rows):
        ref[pl.ds(at + 8 * row, 8), :] = value


def fill_strengths(sides, group, burg, line):
    highs, lows = product_halves(burg, line)
    zero, one = jnp.zeros((8, TILE), F32), jnp.ones((8, TILE), F32)
    at = pl.multiple_of(group * SIDE, SIDE)
    store_rows(sides, at, highs + highs + lows + [zero] * 5)
    store_rows(sides, at + 41 * 8, [one] * 3 + [zero] * 4)


def fill_places(sides, group, places):
    at = pl.multiple_of(group * SIDE, SIDE)
    store_rows(sides, at + 32 * 8, [piece for place in places for piece in pieces_of(place)])


def fill_across_strengths(across, group, burg, line):
    highs, lows = product_halves(burg, line)
    zero = jnp.zeros((8, TILE), F32)
    store_rows(across, group * ACROSS, highs + lows + highs + [zero] * 5)


def fill_across_places(across, group, places):
    zero, one = jnp.zeros((8, TILE), F32), jnp.ones((8, TILE), F32)
    for row in range(3):
        signs = [-one if at // 3 == row else zero for at in range(9)]
        store_rows(
            across,
            group * ACROSS + (32 + 16 * row) * 8,
            signs + pieces_of(places[row]) + [zero] * 4,
        )


def fill_targets(across, targets, strengths):
    def fill(tile, carry):
        at = tile // 8 * ACROSS + tile % 8
        if strengths:
            top = across[pl.ds(at, 32, stride=8), :]
            zero = jnp.zeros((32, 3 * TILE), F32)
            targets[tile, pl.ds(0, 32), :] = jnp.concatenate([top, zero], axis=1).astype(BF16)
        low = [across[pl.ds(at + (32 + 16 * row) * 8, 16, stride=8), :] for row in range(3)]
        low = jnp.concatenate([jnp.zeros((16, TILE), F32)] + low, axis=1)
        targets[tile, pl.ds(32, 16), :] = low.astype(BF16)
        return carry

    lax.fori_loop(0, SEG // TILE, fill, 0)


def near_pass(sweep, live, target_ref, from_ref, target_row, group_row, sides, targets, pairs, near):
    def forces_of_pair(pair):
        source = from_ref[pair]
        left = sides[pl.ds((source >> 3) * SIDE + (source & 7), 48, stride=8), :]
        both = lax.dot_general(
            left.astype(BF16), targets[target_ref[pair]], TN, preferred_element_type=F32
        )
        totals = [jnp.zeros((8, TILE), F32)] * 3
        for chunk in range(16):
            span = both[8 * chunk : 8 * chunk + 8]
            gaps = [span[:, TILE * (row + 1) : TILE * (row + 2)] for row in range(3)]
            radius2 = gaps[0] * gaps[0] + gaps[1] * gaps[1] + gaps[2] * gaps[2] + CORE2
            inverse = lax.rsqrt(radius2)
            weight = span[:, :TILE] * (inverse * inverse * inverse)
            totals = [total + weight * gap for total, gap in zip(totals, gaps)]
        return totals

    def step(block, carry):
        results = [forces_of_pair(block * UNROLL + at) for at in range(UNROLL)]
        for row in range(3):
            rows = [jnp.sum(totals[row], axis=0, keepdims=True) for totals in results]
            at = pl.multiple_of(row * PAIRS + block * UNROLL, UNROLL)
            pairs[pl.ds(at, UNROLL), :] = jnp.concatenate(rows, axis=0)
        return carry

    lax.fori_loop(0, PAIRS // UNROLL, step, 0)
    tile_ids = lax.broadcasted_iota(jnp.int32, (SEG // TILE, PAIRS), 0)
    pair_ids = lax.broadcasted_iota(jnp.int32, (SEG // TILE, PAIRS), 1)
    wanted = (tile_ids == target_row) & (group_row == sweep) & (pair_ids < live)
    select = jnp.where(wanted, 1.0, 0.0).astype(BF16)
    for row in range(3):
        total = None
        for piece in pieces_of(pairs[pl.ds(row * PAIRS, PAIRS), :]):
            part = jnp.dot(select, piece.astype(BF16), preferred_element_type=F32)
            total = part if total is None else total + part
        near[pl.ds(32 * row, 32), :] = total


def step_kernel(
    sizes,
    ghost_hbm,
    live_hbm,
    count_hbm,
    target_scalars,
    from_hbm,
    rel_hbm,
    burg_hbm,
    line_hbm,
    cell_hbm,
    dest_hbm,
    target_hbm,
    group_hbm,
    moved_hbm,
    nodes_hbm,
    ghost_ref,
    live_ref,
    count_ref,
    target_ref,
    from_ref,
    moved_ref,
    nodes_ref,
    rel_ref,
    burg_ref,
    line_ref,
    cell_ref,
    dest_ref,
    target_row,
    group_row,
    own,
    base,
    offset,
    force,
    far,
    payload,
    landing,
    payload_next,
    landing_next,
    mono,
    symm,
    gathered,
    contrib,
    arrived,
    table_ref,
    sides,
    across,
    targets,
    pairs,
    near,
    values,
    lowers,
    centre,
    sums,
    leaving,
    landed,
    load_sem,
    out_sem,
    ghost_send,
    ghost_recv,
    next_send,
    next_recv,
    node_send,
    node_recv,
    plane_send,
    plane_recv,
    line_send,
    line_recv,
):
    loads = [
        pltpu.make_async_copy(source, target, load_sem.at[at])
        for at, (source, target) in enumerate(
            [
                (ghost_hbm, ghost_ref),
                (live_hbm, live_ref),
                (count_hbm, count_ref),
                (target_scalars, target_ref),
                (from_hbm, from_ref),
                (rel_hbm, rel_ref),
                (burg_hbm, burg_ref),
                (line_hbm, line_ref),
                (cell_hbm, cell_ref),
                (dest_hbm, dest_ref),
                (target_hbm, target_row),
                (group_hbm, group_row),
            ]
        )
    ]
    for load in loads:
        load.start()
    nx, ny, nz = sizes
    plane = ny * nz
    place = Place(sizes)
    gx, gy, gz = place.at
    here = gy * nz + gz

    def plane_peer(step):
        peer = here + step
        peer = jnp.where(peer >= plane, peer - plane, peer)
        row = sum((peer >= nz * at).astype(jnp.int32) for at in range(1, ny))
        return (gx, row, peer - nz * row)

    def line_peer(step):
        there = gx + step
        return (jnp.where(there >= nx, there - nx, there), gy, gz)

    barrier = pltpu.get_barrier_semaphore()
    greet_neighbours(place, barrier)

    def greet_plane(step, carry):
        pl.semaphore_signal(barrier, inc=1, device_id=plane_peer(step), device_id_type=MESH)
        return carry

    def greet_line(step, carry):
        pl.semaphore_signal(barrier, inc=1, device_id=line_peer(step), device_id_type=MESH)
        return carry

    lax.fori_loop(1, plane, greet_plane, 0)
    lax.fori_loop(1, nx, greet_line, 0)

    for load in loads:
        load.wait()
    for tile in range(SEG // TILE):
        lanes = pl.ds(tile * TILE, TILE)
        for row in range(3):
            own[tile // 8, row, pl.ds(tile % 8, 1), :] = rel_ref[pl.ds(row, 1), lanes]
            own[tile // 8, 3 + row, pl.ds(tile % 8, 1), :] = burg_ref[pl.ds(row, 1), lanes]
            own[tile // 8, 6 + row, pl.ds(tile % 8, 1), :] = line_ref[pl.ds(row, 1), lanes]
    for group in range(GROUPS):
        rows = slice(8 * group, 8 * group + 8)
        cell = cell_ref[rows, :]
        rel = [own[group, row] for row in range(3)]
        burg = [own[group, 3 + row] for row in range(3)]
        line = [own[group, 6 + row] for row in range(3)]
        corner = (
            jnp.full((8, TILE), gx, jnp.int32),
            gy * 4 + (cell >> 2),
            gz * 4 + (cell & 3),
        )
        for row in range(3):
            corner_row = corner[row].astype(F32) + 0.5
            base[group, row] = corner_row
            offset[group, row] = rel[row]
            own[group, row] = corner_row + rel[row]
        for at, value in enumerate(symmetric(burg, line)):
            symm[pl.ds(at * 32 + 8 * group, 8), :] = value
        u, v, w = (powers(2.0 * value) for value in rel)
        for at, exps in enumerate(EXPONENTS):
            value = monomial(u, v, w, exps)
            mono[pl.ds(at * 32 + 8 * group, 8), :] = (
                jnp.ones((8, TILE), F32) if value is None else value
            )
    for at in range(TERMS, 40):
        mono[pl.ds(at * 32, 32), :] = jnp.zeros((32, TILE), F32)
    for ghost in range(GHOST_DEV):
        tile = ghost_ref[ghost]
        live = jnp.where(ghost < live_ref[0], 1.0, 0.0)
        for row in range(9):
            value = own[tile // 8, row, pl.ds(lax.rem(tile, 8), 1), :]
            payload[row, pl.ds(ghost, 1), :] = value * live

    cells = lax.broadcasted_iota(jnp.int32, (CELL_DEV, TILE), 0)
    moments = jnp.zeros((COMP * CELL_DEV, 40), F32)
    for block in range(4):
        lefts, rights = [], []
        for tile in range(8 * block, 8 * block + 8):
            chosen = cells == cell_ref[pl.ds(tile, 1), :]
            left = jnp.concatenate(
                [
                    jnp.where(chosen, symm[pl.ds(at * 32 + tile, 1), :], 0.0)
                    for at in range(COMP)
                ],
                axis=0,
            )
            right = mono[pl.ds(tile, 40, stride=32), :]
            left_high, left_low = halves_of(left)
            right_high, right_low = halves_of(right)
            lefts += [left_high, left_high, left_low]
            rights += [right_high, right_low, right_high]
        moments = moments + lax.dot_general(
            jnp.concatenate(lefts, axis=1).astype(BF16),
            jnp.concatenate(rights, axis=1).astype(BF16),
            NT,
            preferred_element_type=F32,
        )
    wide = jnp.concatenate([moments, jnp.zeros((COMP * CELL_DEV, TILE - 40), F32)], axis=1)
    mine = pl.ds(pl.multiple_of(here * CELL_DEV, CELL_DEV), CELL_DEV)
    for half in range(2):
        total = jnp.zeros((CELL_DEV, TILE), F32)
        for third in range(3):
            at = (3 * half + third) * CELL_DEV
            part = wide[at : at + CELL_DEV]
            total = total + (pltpu.roll(part, third * LANE_STEP, 1) if third else part)
        gathered[mine, pl.ds(half * TILE, TILE)] = total

    pl.semaphore_wait(barrier, place.count_beside() + plane - 1 + nx - 1)

    def plane_copy(step):
        return pltpu.make_async_remote_copy(
            src_ref=gathered.at[mine],
            dst_ref=gathered.at[mine],
            send_sem=plane_send.at[step],
            recv_sem=plane_recv.at[step],
            device_id=plane_peer(step),
            device_id_type=MESH,
        )

    toward = 1 - 2 * lax.rem(gy, 2)

    def slot_of(step_x, step_y, step_z):
        return (step_x + 1) * 9 + (step_y + 1) * 3 + step_z + 1

    def ghost_copy(source, where, slot, at):
        return pltpu.make_async_remote_copy(
            src_ref=source,
            dst_ref=landing.at[slot],
            send_sem=ghost_send.at[at],
            recv_sem=ghost_recv.at[slot],
            device_id=where,
            device_id_type=MESH,
        )

    def level_copy(step_x, step_z):
        return ghost_copy(
            payload,
            (gx + step_x, gy, gz + step_z),
            slot_of(-step_x, 0, -step_z),
            slot_of(step_x, 0, step_z),
        )

    def partner_copy():
        return ghost_copy(payload, (gx, gy + toward, gz), slot_of(0, -toward, 0), 13)

    def away_copy(step_x, step_z):
        return ghost_copy(
            payload,
            (gx + step_x, gy - toward, gz + step_z),
            slot_of(-step_x, toward, -step_z),
            slot_of(step_x, -1, step_z),
        )

    def handed_copy(step_x, step_z):
        return ghost_copy(
            landing.at[slot_of(step_x, 0, step_z)],
            (gx, gy + toward, gz),
            slot_of(step_x, -toward, step_z),
            slot_of(step_x, 1, step_z),
        )

    def each_level(body, centre=False):
        for step_x in (-1, 0, 1):
            for step_z in (-1, 0, 1):
                if centre or step_x or step_z:
                    pl.when(place.inside(step_x, step_z))(
                        functools.partial(body, step_x, step_z)
                    )

    def each_away(body):
        @pl.when(jnp.logical_and(gy - toward >= 0, gy - toward < ny))
        def _():
            each_level(body, True)

    def start_plane(step, carry):
        plane_copy(step).start()
        return carry

    lax.fori_loop(1, plane, start_plane, 0)

    each_level(lambda x, z: level_copy(x, z).start())
    partner_copy().start()
    each_away(lambda x, z: away_copy(x, z).start())

    def clear(slot):
        _, inside = place.beside(slot)

        @pl.when(jnp.logical_not(inside))
        def _():
            landing[slot] = jnp.zeros((9, GHOST_DEV, TILE), F32)
            landing_next[slot] = jnp.zeros((3, GHOST_DEV, TILE), F32)
            landed[slot] = jnp.zeros((3, 8, TILE), F32)

    each_slot(clear)
    landing[13] = jnp.zeros((9, GHOST_DEV, TILE), F32)
    landing_next[13] = jnp.zeros((3, GHOST_DEV, TILE), F32)

    for group in range(GROUPS):
        places = [own[group, row] for row in range(3)]
        burg = [own[group, 3 + row] for row in range(3)]
        line = [own[group, 6 + row] for row in range(3)]
        fill_strengths(sides, group, burg, line)
        fill_places(sides, group, places)
        fill_across_strengths(across, group, burg, line)
        fill_across_places(across, group, places)
    fill_targets(across, targets, True)
    rows, columns = nx * CELL_DEV, plane * CELL_DEV
    row = lax.broadcasted_iota(jnp.int32, (rows, columns), 0)
    column = lax.broadcasted_iota(jnp.int32, (rows, columns), 1)
    peer = column >> 4
    step_x = (row >> 4) - gx
    step_y = gy * 4 + ((row >> 2) & 3) - (peer // nz * 4 + ((column >> 2) & 3))
    step_z = gz * 4 + (row & 3) - (peer % nz * 4 + (column & 3))
    distance2 = (step_x * step_x + step_y * step_y + step_z * step_z).astype(F32)
    weight = jnp.where(distance2 > 3.5, 1.0 / jnp.sqrt(jnp.maximum(distance2, 1.0)), 0.0)

    def wait_plane(step, carry):
        plane_copy(step).wait()
        return carry

    lax.fori_loop(1, plane, wait_plane, 0)
    contrib[...] = jnp.dot(
        weight, gathered[...], precision=lax.Precision.HIGHEST, preferred_element_type=F32
    )

    def line_copy(step):
        there = line_peer(step)[0]
        return pltpu.make_async_remote_copy(
            src_ref=contrib.at[pl.ds(pl.multiple_of(there * CELL_DEV, CELL_DEV), CELL_DEV)],
            dst_ref=arrived.at[step],
            send_sem=line_send.at[step],
            recv_sem=line_recv.at[step],
            device_id=line_peer(step),
            device_id_type=MESH,
        )

    def start_line(step, carry):
        line_copy(step).start()
        return carry

    lax.fori_loop(1, nx, start_line, 0)
    def hand_on(step_x, step_z):
        level_copy(-step_x, -step_z).wait_recv()
        handed_copy(step_x, step_z).start()

    def wait_handed(step_x, step_z):
        slot = slot_of(step_x, toward, step_z)
        ghost_copy(payload, place.at, slot, 0).wait_recv()

    def wait_away(step_x, step_z):
        slot = slot_of(step_x, -toward, step_z)
        ghost_copy(payload, place.at, slot, 0).wait_recv()

    each_level(hand_on)
    wait_handed(0, 0)
    each_away(wait_away)
    each_level(wait_handed)

    def take_ghosts(slot, carry):
        block = [landing[slot, row] for row in range(9)]
        fill_strengths(sides, GROUPS + slot, block[3:6], block[6:9])
        fill_places(sides, GROUPS + slot, block[0:3])
        return carry

    lax.fori_loop(0, 27, take_ghosts, 0)
    live = count_ref[0]
    near_pass(
        0, live, target_ref, from_ref, target_row[...], group_row[...], sides, targets, pairs, near
    )
    total = contrib[pl.ds(pl.multiple_of(gx * CELL_DEV, CELL_DEV), CELL_DEV), :]

    def wait_line(step, carry):
        line_copy(step).wait()
        return carry

    lax.fori_loop(1, nx, wait_line, 0)
    for step in range(1, nx):
        total = total + arrived[step]
    full = jnp.concatenate([total, jnp.zeros((TILE - CELL_DEV, 2 * TILE), F32)], axis=0)
    table_ref[pl.ds(0, TILE), :] = full[:, :TILE].T
    table_ref[pl.ds(TILE, TILE), :] = full[:, TILE:].T
    def far_pass(group):
        return far_force(
            [offset[group, row] for row in range(3)],
            [own[group, 3 + row] for row in range(3)],
            [own[group, 6 + row] for row in range(3)],
            cell_ref[pl.ds(8 * group, 8), :],
            table_ref,
        )

    for group in range(GROUPS):
        coupling = far_pass(group)
        for row in range(3):
            total = FAR_SCALE * coupling[row] + NEAR_SCALE * near[pl.ds(32 * row + 8 * group, 8), :]
            moved = offset[group, row] + STEP_SIZE * total
            force[group, row] = total
            offset[group, row] = moved
            own[group, row] = base[group, row] + moved
    for ghost in range(GHOST_DEV):
        tile = ghost_ref[ghost]
        for row in range(3):
            payload_next[row, pl.ds(ghost, 1), :] = own[tile // 8, row, pl.ds(lax.rem(tile, 8), 1), :]
    start_next, wait_next, wait_next_sent = exchange(
        place, lambda slot: payload_next, lambda slot: landing_next.at[slot], next_send, next_recv
    )
    each_slot(start_next)

    for group in range(GROUPS):
        coupling = far_pass(group)
        for row in range(3):
            far[group, row] = coupling[row]
        places = [own[group, row] for row in range(3)]
        fill_places(sides, group, places)
        fill_across_places(across, group, places)
    fill_targets(across, targets, False)
    low_ids = lax.broadcasted_iota(jnp.int32, (256, WIDTH), 0)

    def fill_lowers(block, carry):
        lanes = pl.ds(pl.multiple_of(block * WIDTH, WIDTH), WIDTH)
        for end in range(2):
            lower = dest_ref[pl.ds(end, 1), lanes] & 255
            lowers[block, :, pl.ds(end * WIDTH, WIDTH)] = jnp.where(
                low_ids == lower, 1.0, 0.0
            ).astype(BF16)
        return carry

    lax.fori_loop(0, SEG // WIDTH, fill_lowers, 0)

    def take_next(slot, carry):
        fill_places(sides, GROUPS + slot, [landing_next[slot, row] for row in range(3)])
        return carry

    each_slot(wait_next)
    lax.fori_loop(0, 27, take_next, 0)
    near_pass(
        1, live, target_ref, from_ref, target_row[...], group_row[...], sides, targets, pairs, near
    )
    for group in range(GROUPS):
        for row in range(3):
            total = FAR_SCALE * far[group, row] + NEAR_SCALE * near[pl.ds(32 * row + 8 * group, 8), :]
            moved = offset[group, row] + STEP_SIZE * total
            half = 0.5 * (force[group, row] + total)
            for tile in range(8):
                lanes = pl.ds((8 * group + tile) * TILE, TILE)
                moved_ref[pl.ds(row, 1), lanes] = moved[tile : tile + 1]
                values[pl.ds(row, 1), lanes] = half[tile : tile + 1]

    save_moved = pltpu.make_async_copy(moved_ref, moved_hbm, out_sem.at[0])
    save_moved.start()

    def scatter(first, count, totals):
        totals[...] = jnp.zeros(totals.shape, F32)
        high_ids = lax.broadcasted_iota(jnp.int32, (count, WIDTH), 0) + first

        def add(block, carry):
            lanes = pl.ds(pl.multiple_of(block * WIDTH, WIDTH), WIDTH)
            parts = [halves_of(values[pl.ds(row, 1), lanes]) for row in range(3)]
            lefts = []
            for end in range(2):
                dest = dest_ref[pl.ds(end, 1), lanes]
                slot = dest >> 12
                first_row = jnp.where(slot > 13, 12 + 4 * slot, 16 + 4 * slot)
                upper = jnp.where(slot == 13, 0, first_row) + ((dest & (SEG - 1)) >> 8)
                chosen = high_ids == upper
                lefts.append(
                    [
                        jnp.where(chosen, parts[row][piece], 0.0)
                        for row in range(3)
                        for piece in range(2)
                    ]
                )
            left = jnp.concatenate(
                [jnp.concatenate(both, axis=1) for both in zip(*lefts)], axis=0
            ).astype(BF16)
            totals[...] += lax.dot_general(left, lowers[block], NT, preferred_element_type=F32)
            return carry

        lax.fori_loop(0, SEG // WIDTH, add, 0)

    scatter(16, 104, sums)
    for row in range(3):
        for slot in range(27):
            if slot == 13:
                continue
            at = 208 * row + 4 * (slot - (slot > 13))
            both = sums[pl.ds(at, 4), :] + sums[pl.ds(at + 104, 4), :]
            leaving[slot, row, pl.ds(0, 4), :] = both[:, :TILE]
            leaving[slot, row, pl.ds(4, 4), :] = both[:, TILE:]
    start_node, wait_node, wait_node_sent = exchange(
        place, lambda slot: leaving.at[slot], lambda slot: landed.at[slot], node_send, node_recv
    )
    each_slot(start_node)
    scatter(0, 16, centre)
    middle = [
        centre[pl.ds(32 * row, 16), :] + centre[pl.ds(32 * row + 16, 16), :] for row in range(3)
    ]
    for row in range(3):
        for part in range(4, 16):
            nodes_ref[pl.ds(row, 1), pl.ds(256 * part, 256)] = middle[row][part : part + 1]
    inner = pl.ds(1024, SEG - 1024)
    save_inner = pltpu.make_async_copy(
        nodes_ref.at[:, inner], nodes_hbm.at[:, inner], out_sem.at[1]
    )
    save_inner.start()
    each_slot(wait_node)
    for row in range(3):
        total = landed[0, row]
        for slot in range(1, 27):
            if slot != 13:
                total = total + landed[slot, row]
        for part in range(4):
            for half in range(2):
                lanes = slice(TILE * half, TILE * half + TILE)
                nodes_ref[pl.ds(row, 1), pl.ds(256 * part + TILE * half, TILE)] = (
                    middle[row][part : part + 1, lanes]
                    + total[4 * half + part : 4 * half + part + 1]
                )

    outer = pl.ds(0, 1024)
    save_outer = pltpu.make_async_copy(
        nodes_ref.at[:, outer], nodes_hbm.at[:, outer], out_sem.at[2]
    )
    save_outer.start()

    each_level(lambda x, z: level_copy(x, z).wait_send())
    partner_copy().wait_send()
    each_away(lambda x, z: away_copy(x, z).wait_send())
    each_level(lambda x, z: handed_copy(x, z).wait_send())
    each_slot(wait_next_sent)
    each_slot(wait_node_sent)
    for save in (save_moved, save_inner, save_outer):
        save.wait()


def on_device(
    sizes,
    seg_rel,
    burgers,
    line_vec,
    seg_cell,
    ghost_tiles,
    ghost_count,
    pair_target,
    pair_source,
    pair_group,
    pair_count,
    node_dest,
):
    nx, ny, nz = sizes
    plane = ny * nz
    cell = seg_cell.reshape(SEG // TILE, TILE)
    shape = jax.ShapeDtypeStruct
    dma = pltpu.SemaphoreType.DMA
    block = (GROUPS, 3, 8, TILE)
    buffers = [
        (3, SEG),
        (3, SEG),
        (3, SEG),
        (3, SEG),
        (3, SEG),
        (SEG // TILE, TILE, jnp.int32),
        (2, SEG, jnp.int32),
        (1, PAIRS, jnp.int32),
        (1, PAIRS, jnp.int32),
        (GROUPS, 9, 8, TILE),
        block,
        block,
        block,
        block,
        (9, GHOST_DEV, TILE),
        (27, 9, GHOST_DEV, TILE),
        (3, GHOST_DEV, TILE),
        (27, 3, GHOST_DEV, TILE),
        (40 * 32, TILE),
        (COMP * 32, TILE),
        (plane * CELL_DEV, 2 * TILE),
        (nx * CELL_DEV, 2 * TILE),
        (nx, CELL_DEV, 2 * TILE),
        (2 * TILE, TILE),
        ((GROUPS + 27) * SIDE, TILE),
        (GROUPS * ACROSS, TILE),
        (SEG // TILE, 48, 4 * TILE, BF16),
        (3 * PAIRS, TILE),
        (3 * SEG // TILE, TILE),
        (8, SEG),
        (SEG // WIDTH, 256, 2 * WIDTH, BF16),
        (96, 256),
        (624, 256),
        (27, 3, 8, TILE),
        (27, 3, 8, TILE),
    ]
    scratch = []
    for sides in buffers:
        kind = F32
        if not isinstance(sides[-1], int):
            sides, kind = sides[:-1], sides[-1]
        scratch.append(pltpu.VMEM(sides, kind))
    return pl.pallas_call(
        functools.partial(step_kernel, sizes),
        out_shape=(shape((3, SEG), F32), shape((3, SEG), F32)),
        in_specs=[pl.BlockSpec(memory_space=pl.ANY)] * 12,
        out_specs=(pl.BlockSpec(memory_space=pl.ANY),) * 2,
        scratch_shapes=[
            pltpu.SMEM((count,), jnp.int32) for count in (GHOST_DEV, 1, 1, PAIRS, PAIRS)
        ]
        + scratch
        + [dma((12,)), dma((3,))]
        + [dma((27,))] * 6
        + [dma((plane,))] * 2
        + [dma((nx,))] * 2,
        compiler_params=pltpu.CompilerParams(
            collective_id=0, has_side_effects=True, vmem_limit_bytes=56 << 20
        ),
        name="step",
    )(
        ghost_tiles,
        ghost_count,
        pair_count,
        pair_target,
        pair_source,
        seg_rel,
        burgers,
        line_vec,
        cell,
        node_dest,
        pair_target.reshape(1, PAIRS),
        pair_group.reshape(1, PAIRS),
    )


def solution(mesh):
    sizes = tuple(mesh.shape[name] for name in ("gx", "gy", "gz"))
    whole = ("gx", "gy", "gz")
    return jax.shard_map(
        functools.partial(on_device, sizes),
        mesh=mesh,
        in_specs=(P(None, whole),) * 3 + (P(whole),) * 7 + (P(None, whole),),
        out_specs=(P(None, whole), P(None, whole)),
        check_vma=False,
    )
```

```python
import functools

import jax
import jax.numpy as jnp
from jax import lax
from jax.experimental import pallas as pl
from jax.experimental.pallas import tpu as pltpu
from jax.sharding import PartitionSpec as P

TILE = 128
SEG = 4096
GROUPS = 4
GHOST_DEV = 8
CELL_DEV = 16
COMP = 6
TERMS = 35
LANE_STEP = 42
PAIRS = 128
CORE2 = 0.25
NEAR_SCALE = 0.05
FAR_SCALE = 0.002
STEP_SIZE = 0.1
MESH = pl.DeviceIdType.MESH
F32 = jnp.float32
BF16 = jnp.bfloat16
EXPONENTS = [
    (a, b, degree - a - b)
    for degree in range(5)
    for a in range(degree, -1, -1)
    for b in range(degree - a, -1, -1)
]
NT = (((1,), (1,)), ((), ()))
TN = (((0,), (0,)), ((), ()))


def vmem(count):
    return [pl.BlockSpec(memory_space=pltpu.VMEM)] * count


def smem(count):
    return [pl.BlockSpec(memory_space=pltpu.SMEM)] * count


def halves_of(value):
    high = value.astype(BF16).astype(F32)
    return high, value - high


def powers(unit):
    square = unit * unit
    return [None, unit, square, square * unit, square * square]


def monomial(u, v, w, exps):
    result = None
    for table, power in zip((u, v, w), exps):
        if power:
            result = table[power] if result is None else result * table[power]
    return result


def symmetric(b, t):
    return [
        b[0] * t[0],
        b[1] * t[1],
        b[2] * t[2],
        0.5 * (b[0] * t[1] + b[1] * t[0]),
        0.5 * (b[1] * t[2] + b[2] * t[1]),
        0.5 * (b[0] * t[2] + b[2] * t[0]),
    ]


class Place:
    def __init__(self, sizes):
        self.sizes = sizes
        self.at = tuple(lax.axis_index(name) for name in ("gx", "gy", "gz"))
        self.free = [
            {-1: at > 0, 1: at < size - 1} for at, size in zip(self.at, sizes)
        ]

    def beside(self, slot):
        steps = (slot // 9 - 1, slot // 3 % 3 - 1, slot % 3 - 1)
        where = tuple(at + step for at, step in zip(self.at, steps))
        inside = None
        for free, step in zip(self.free, steps):
            if step:
                inside = free[step] if inside is None else jnp.logical_and(inside, free[step])
        return where, inside

    def inside(self, step_x, step_z):
        found = True
        for free, step in ((self.free[0], step_x), (self.free[2], step_z)):
            if step:
                found = free[step] if found is True else jnp.logical_and(found, free[step])
        return found

    def count_beside(self):
        total = 1
        for at, size in zip(self.at, self.sizes):
            total = total * (3 - (at == 0).astype(jnp.int32) - (at == size - 1).astype(jnp.int32))
        return total - 1


SLOTS = sorted(
    (slot for slot in range(27) if slot != 13),
    key=lambda slot: (slot // 9 == 1) + (slot // 3 % 3 == 1) + (slot % 3 == 1),
)


def each_slot(body):
    for slot in SLOTS:
        body(slot)


def greet_neighbours(place, barrier):
    def greet(slot):
        where, inside = place.beside(slot)

        @pl.when(inside)
        def _():
            pl.semaphore_signal(barrier, inc=1, device_id=where, device_id_type=MESH)

    each_slot(greet)


def far_force(offset, burg, line, cell, table_ref):
    u, v, w = (powers(2.0 * value) for value in offset)
    stress = [None] * COMP
    for at, exps in enumerate(EXPONENTS):
        value = monomial(u, v, w, exps)
        for comp in range(COMP):
            row = comp // 3 * TILE + comp % 3 * LANE_STEP + at
            entry = jnp.broadcast_to(table_ref[pl.ds(row, 1), :], (8, TILE))
            term = jnp.take_along_axis(entry, cell, axis=1, mode="promise_in_bounds")
            if value is not None:
                term = term * value
            stress[comp] = term if stress[comp] is None else stress[comp] + term
    push_x = stress[0] * burg[0] + stress[3] * burg[1] + stress[5] * burg[2]
    push_y = stress[3] * burg[0] + stress[1] * burg[1] + stress[4] * burg[2]
    push_z = stress[5] * burg[0] + stress[4] * burg[1] + stress[2] * burg[2]
    return [
        push_y * line[2] - push_z * line[1],
        push_z * line[0] - push_x * line[2],
        push_x * line[1] - push_y * line[0],
    ]


def exchange(place, send_of, receive_at, send_sem, recv_sem):
    def copy_of(slot):
        where, inside = place.beside(slot)
        copy = pltpu.make_async_remote_copy(
            src_ref=send_of(slot),
            dst_ref=receive_at(26 - slot),
            send_sem=send_sem.at[slot],
            recv_sem=recv_sem.at[26 - slot],
            device_id=where,
            device_id_type=MESH,
        )
        return copy, inside

    def start(slot):
        copy, inside = copy_of(slot)

        @pl.when(inside)
        def _():
            copy.start()

    def wait(slot):
        arriving, _ = copy_of(26 - slot)
        _, inside = place.beside(slot)

        @pl.when(inside)
        def _():
            arriving.wait_recv()

    def wait_sent(slot):
        copy, inside = copy_of(slot)

        @pl.when(inside)
        def _():
            copy.wait_send()

    return start, wait, wait_sent


SIDE = 48 * 8
ACROSS = 80 * 8
UNROLL = 32
WIDTH = 512


def pieces_of(value):
    high = value.astype(BF16).astype(F32)
    rest = value - high
    middle = rest.astype(BF16).astype(F32)
    return [high, middle, rest - middle]


def product_halves(burg, line):
    highs, lows = [], []
    for b in burg:
        for t in line:
            high, low = halves_of(b * t)
            highs.append(high)
            lows.append(low)
    return highs, lows


def store_rows(ref, at, rows):
    for row, value in enumerate(rows):
        ref[pl.ds(at + 8 * row, 8), :] = value


def fill_strengths(sides, group, burg, line):
    highs, lows = product_halves(burg, line)
    zero, one = jnp.zeros((8, TILE), F32), jnp.ones((8, TILE), F32)
    at = pl.multiple_of(group * SIDE, SIDE)
    store_rows(sides, at, highs + highs + lows + [zero] * 5)
    store_rows(sides, at + 41 * 8, [one] * 3 + [zero] * 4)


def fill_places(sides, group, places):
    at = pl.multiple_of(group * SIDE, SIDE)
    store_rows(sides, at + 32 * 8, [piece for place in places for piece in pieces_of(place)])


def fill_across_strengths(across, group, burg, line):
    highs, lows = product_halves(burg, line)
    zero = jnp.zeros((8, TILE), F32)
    store_rows(across, group * ACROSS, highs + lows + highs + [zero] * 5)


def fill_across_places(across, group, places):
    zero, one = jnp.zeros((8, TILE), F32), jnp.ones((8, TILE), F32)
    for row in range(3):
        signs = [-one if at // 3 == row else zero for at in range(9)]
        store_rows(
            across,
            group * ACROSS + (32 + 16 * row) * 8,
            signs + pieces_of(places[row]) + [zero] * 4,
        )


def fill_targets(across, targets, strengths):
    def fill(tile, carry):
        at = tile // 8 * ACROSS + tile % 8
        if strengths:
            top = across[pl.ds(at, 32, stride=8), :]
            zero = jnp.zeros((32, 3 * TILE), F32)
            targets[tile, pl.ds(0, 32), :] = jnp.concatenate([top, zero], axis=1).astype(BF16)
        low = [across[pl.ds(at + (32 + 16 * row) * 8, 16, stride=8), :] for row in range(3)]
        low = jnp.concatenate([jnp.zeros((16, TILE), F32)] + low, axis=1)
        targets[tile, pl.ds(32, 16), :] = low.astype(BF16)
        return carry

    lax.fori_loop(0, SEG // TILE, fill, 0)


def near_pass(sweep, live, target_ref, from_ref, target_row, group_row, sides, targets, pairs, near):
    def forces_of_pair(pair):
        source = from_ref[pair]
        left = sides[pl.ds((source >> 3) * SIDE + (source & 7), 48, stride=8), :]
        both = lax.dot_general(
            left.astype(BF16), targets[target_ref[pair]], TN, preferred_element_type=F32
        )
        totals = [jnp.zeros((8, TILE), F32)] * 3
        for chunk in range(16):
            span = both[8 * chunk : 8 * chunk + 8]
            gaps = [span[:, TILE * (row + 1) : TILE * (row + 2)] for row in range(3)]
            radius2 = gaps[0] * gaps[0] + gaps[1] * gaps[1] + gaps[2] * gaps[2] + CORE2
            inverse = lax.rsqrt(radius2)
            weight = span[:, :TILE] * (inverse * inverse * inverse)
            totals = [total + weight * gap for total, gap in zip(totals, gaps)]
        return totals

    def step(block, carry):
        results = [forces_of_pair(block * UNROLL + at) for at in range(UNROLL)]
        for row in range(3):
            rows = [jnp.sum(totals[row], axis=0, keepdims=True) for totals in results]
            at = pl.multiple_of(row * PAIRS + block * UNROLL, UNROLL)
            pairs[pl.ds(at, UNROLL), :] = jnp.concatenate(rows, axis=0)
        return carry

    lax.fori_loop(0, PAIRS // UNROLL, step, 0)
    tile_ids = lax.broadcasted_iota(jnp.int32, (SEG // TILE, PAIRS), 0)
    pair_ids = lax.broadcasted_iota(jnp.int32, (SEG // TILE, PAIRS), 1)
    wanted = (tile_ids == target_row) & (group_row == sweep) & (pair_ids < live)
    select = jnp.where(wanted, 1.0, 0.0).astype(BF16)
    for row in range(3):
        total = None
        for piece in pieces_of(pairs[pl.ds(row * PAIRS, PAIRS), :]):
            part = jnp.dot(select, piece.astype(BF16), preferred_element_type=F32)
            total = part if total is None else total + part
        near[pl.ds(32 * row, 32), :] = total


def step_kernel(
    sizes,
    ghost_hbm,
    live_hbm,
    count_hbm,
    target_scalars,
    from_hbm,
    rel_hbm,
    burg_hbm,
    line_hbm,
    cell_hbm,
    dest_hbm,
    target_hbm,
    group_hbm,
    moved_hbm,
    nodes_hbm,
    ghost_ref,
    live_ref,
    count_ref,
    target_ref,
    from_ref,
    moved_ref,
    nodes_ref,
    rel_ref,
    burg_ref,
    line_ref,
    cell_ref,
    dest_ref,
    target_row,
    group_row,
    own,
    base,
    offset,
    force,
    far,
    payload,
    landing,
    payload_next,
    landing_next,
    mono,
    symm,
    gathered,
    contrib,
    arrived,
    table_ref,
    sides,
    across,
    targets,
    pairs,
    near,
    values,
    lowers,
    centre,
    sums,
    leaving,
    landed,
    load_sem,
    out_sem,
    ghost_send,
    ghost_recv,
    next_send,
    next_recv,
    node_send,
    node_recv,
    plane_send,
    plane_recv,
    line_send,
    line_recv,
):
    loads = [
        pltpu.make_async_copy(source, target, load_sem.at[at])
        for at, (source, target) in enumerate(
            [
                (ghost_hbm, ghost_ref),
                (live_hbm, live_ref),
                (count_hbm, count_ref),
                (target_scalars, target_ref),
                (from_hbm, from_ref),
                (rel_hbm, rel_ref),
                (burg_hbm, burg_ref),
                (line_hbm, line_ref),
                (cell_hbm, cell_ref),
                (dest_hbm, dest_ref),
                (target_hbm, target_row),
                (group_hbm, group_row),
            ]
        )
    ]
    for load in loads:
        load.start()
    nx, ny, nz = sizes
    plane = ny * nz
    place = Place(sizes)
    gx, gy, gz = place.at
    here = gy * nz + gz

    def plane_peer(step):
        peer = here + step
        peer = jnp.where(peer >= plane, peer - plane, peer)
        row = sum((peer >= nz * at).astype(jnp.int32) for at in range(1, ny))
        return (gx, row, peer - nz * row)

    def line_peer(step):
        there = gx + step
        return (jnp.where(there >= nx, there - nx, there), gy, gz)

    barrier = pltpu.get_barrier_semaphore()
    greet_neighbours(place, barrier)

    def greet_plane(step, carry):
        pl.semaphore_signal(barrier, inc=1, device_id=plane_peer(step), device_id_type=MESH)
        return carry

    def greet_line(step, carry):
        pl.semaphore_signal(barrier, inc=1, device_id=line_peer(step), device_id_type=MESH)
        return carry

    lax.fori_loop(1, plane, greet_plane, 0)
    lax.fori_loop(1, nx, greet_line, 0)

    for load in loads:
        load.wait()
    for tile in range(SEG // TILE):
        lanes = pl.ds(tile * TILE, TILE)
        for row in range(3):
            own[tile // 8, row, pl.ds(tile % 8, 1), :] = rel_ref[pl.ds(row, 1), lanes]
            own[tile // 8, 3 + row, pl.ds(tile % 8, 1), :] = burg_ref[pl.ds(row, 1), lanes]
            own[tile // 8, 6 + row, pl.ds(tile % 8, 1), :] = line_ref[pl.ds(row, 1), lanes]
    for group in range(GROUPS):
        rows = slice(8 * group, 8 * group + 8)
        cell = cell_ref[rows, :]
        rel = [own[group, row] for row in range(3)]
        burg = [own[group, 3 + row] for row in range(3)]
        line = [own[group, 6 + row] for row in range(3)]
        corner = (
            jnp.full((8, TILE), gx, jnp.int32),
            gy * 4 + (cell >> 2),
            gz * 4 + (cell & 3),
        )
        for row in range(3):
            corner_row = corner[row].astype(F32) + 0.5
            base[group, row] = corner_row
            offset[group, row] = rel[row]
            own[group, row] = corner_row + rel[row]
        for at, value in enumerate(symmetric(burg, line)):
            symm[pl.ds(at * 32 + 8 * group, 8), :] = value
        u, v, w = (powers(2.0 * value) for value in rel)
        for at, exps in enumerate(EXPONENTS):
            value = monomial(u, v, w, exps)
            mono[pl.ds(at * 32 + 8 * group, 8), :] = (
                jnp.ones((8, TILE), F32) if value is None else value
            )
    for at in range(TERMS, 40):
        mono[pl.ds(at * 32, 32), :] = jnp.zeros((32, TILE), F32)
    for ghost in range(GHOST_DEV):
        tile = ghost_ref[ghost]
        live = jnp.where(ghost < live_ref[0], 1.0, 0.0)
        for row in range(9):
            value = own[tile // 8, row, pl.ds(lax.rem(tile, 8), 1), :]
            payload[row, pl.ds(ghost, 1), :] = value * live

    cells = lax.broadcasted_iota(jnp.int32, (CELL_DEV, TILE), 0)
    moments = jnp.zeros((COMP * CELL_DEV, 40), F32)
    for block in range(4):
        lefts, rights = [], []
        for tile in range(8 * block, 8 * block + 8):
            chosen = cells == cell_ref[pl.ds(tile, 1), :]
            left = jnp.concatenate(
                [
                    jnp.where(chosen, symm[pl.ds(at * 32 + tile, 1), :], 0.0)
                    for at in range(COMP)
                ],
                axis=0,
            )
            right = mono[pl.ds(tile, 40, stride=32), :]
            left_high, left_low = halves_of(left)
            right_high, right_low = halves_of(right)
            lefts += [left_high, left_high, left_low]
            rights += [right_high, right_low, right_high]
        moments = moments + lax.dot_general(
            jnp.concatenate(lefts, axis=1).astype(BF16),
            jnp.concatenate(rights, axis=1).astype(BF16),
            NT,
            preferred_element_type=F32,
        )
    wide = jnp.concatenate([moments, jnp.zeros((COMP * CELL_DEV, TILE - 40), F32)], axis=1)
    mine = pl.ds(pl.multiple_of(here * CELL_DEV, CELL_DEV), CELL_DEV)
    for half in range(2):
        total = jnp.zeros((CELL_DEV, TILE), F32)
        for third in range(3):
            at = (3 * half + third) * CELL_DEV
            part = wide[at : at + CELL_DEV]
            total = total + (pltpu.roll(part, third * LANE_STEP, 1) if third else part)
        gathered[mine, pl.ds(half * TILE, TILE)] = total

    pl.semaphore_wait(barrier, place.count_beside() + plane - 1 + nx - 1)

    def plane_copy(step):
        return pltpu.make_async_remote_copy(
            src_ref=gathered.at[mine],
            dst_ref=gathered.at[mine],
            send_sem=plane_send.at[step],
            recv_sem=plane_recv.at[step],
            device_id=plane_peer(step),
            device_id_type=MESH,
        )

    toward = 1 - 2 * lax.rem(gy, 2)

    def slot_of(step_x, step_y, step_z):
        return (step_x + 1) * 9 + (step_y + 1) * 3 + step_z + 1

    def ghost_copy(source, where, slot, at):
        return pltpu.make_async_remote_copy(
            src_ref=source,
            dst_ref=landing.at[slot],
            send_sem=ghost_send.at[at],
            recv_sem=ghost_recv.at[slot],
            device_id=where,
            device_id_type=MESH,
        )

    def level_copy(step_x, step_z):
        return ghost_copy(
            payload,
            (gx + step_x, gy, gz + step_z),
            slot_of(-step_x, 0, -step_z),
            slot_of(step_x, 0, step_z),
        )

    def partner_copy():
        return ghost_copy(payload, (gx, gy + toward, gz), slot_of(0, -toward, 0), 13)

    def away_copy(step_x, step_z):
        return ghost_copy(
            payload,
            (gx + step_x, gy - toward, gz + step_z),
            slot_of(-step_x, toward, -step_z),
            slot_of(step_x, -1, step_z),
        )

    def handed_copy(step_x, step_z):
        return ghost_copy(
            landing.at[slot_of(step_x, 0, step_z)],
            (gx, gy + toward, gz),
            slot_of(step_x, -toward, step_z),
            slot_of(step_x, 1, step_z),
        )

    def each_level(body, centre=False):
        for step_x in (-1, 0, 1):
            for step_z in (-1, 0, 1):
                if centre or step_x or step_z:
                    pl.when(place.inside(step_x, step_z))(
                        functools.partial(body, step_x, step_z)
                    )

    def hand_on(step_x, step_z):
        level_copy(-step_x, -step_z).wait_recv()
        handed_copy(step_x, step_z).start()

    def each_away(body):
        @pl.when(jnp.logical_and(gy - toward >= 0, gy - toward < ny))
        def _():
            each_level(body, True)

    def start_plane(step, carry):
        plane_copy(step).start()
        return carry

    lax.fori_loop(1, plane, start_plane, 0)

    each_level(lambda x, z: level_copy(x, z).start())
    partner_copy().start()
    each_away(lambda x, z: away_copy(x, z).start())

    def clear(slot):
        _, inside = place.beside(slot)

        @pl.when(jnp.logical_not(inside))
        def _():
            landing[slot] = jnp.zeros((9, GHOST_DEV, TILE), F32)
            landing_next[slot] = jnp.zeros((3, GHOST_DEV, TILE), F32)
            landed[slot] = jnp.zeros((3, 8, TILE), F32)

    each_slot(clear)
    landing[13] = jnp.zeros((9, GHOST_DEV, TILE), F32)
    landing_next[13] = jnp.zeros((3, GHOST_DEV, TILE), F32)

    for group in range(GROUPS):
        places = [own[group, row] for row in range(3)]
        burg = [own[group, 3 + row] for row in range(3)]
        line = [own[group, 6 + row] for row in range(3)]
        fill_strengths(sides, group, burg, line)
        fill_places(sides, group, places)
        fill_across_strengths(across, group, burg, line)
        fill_across_places(across, group, places)
    fill_targets(across, targets, True)
    rows, columns = nx * CELL_DEV, plane * CELL_DEV
    row = lax.broadcasted_iota(jnp.int32, (rows, columns), 0)
    column = lax.broadcasted_iota(jnp.int32, (rows, columns), 1)
    peer = column >> 4
    step_x = (row >> 4) - gx
    step_y = gy * 4 + ((row >> 2) & 3) - (peer // nz * 4 + ((column >> 2) & 3))
    step_z = gz * 4 + (row & 3) - (peer % nz * 4 + (column & 3))
    distance2 = (step_x * step_x + step_y * step_y + step_z * step_z).astype(F32)
    weight = jnp.where(distance2 > 3.5, 1.0 / jnp.sqrt(jnp.maximum(distance2, 1.0)), 0.0)

    def wait_plane(step, carry):
        plane_copy(step).wait()
        return carry

    lax.fori_loop(1, plane, wait_plane, 0)
    each_level(hand_on)
    contrib[...] = jnp.dot(
        weight, gathered[...], precision=lax.Precision.HIGHEST, preferred_element_type=F32
    )

    def line_copy(step):
        there = line_peer(step)[0]
        return pltpu.make_async_remote_copy(
            src_ref=contrib.at[pl.ds(pl.multiple_of(there * CELL_DEV, CELL_DEV), CELL_DEV)],
            dst_ref=arrived.at[step],
            send_sem=line_send.at[step],
            recv_sem=line_recv.at[step],
            device_id=line_peer(step),
            device_id_type=MESH,
        )

    def start_line(step, carry):
        line_copy(step).start()
        return carry

    lax.fori_loop(1, nx, start_line, 0)
    def wait_handed(step_x, step_z):
        slot = slot_of(step_x, toward, step_z)
        ghost_copy(payload, place.at, slot, 0).wait_recv()

    def wait_away(step_x, step_z):
        slot = slot_of(step_x, -toward, step_z)
        ghost_copy(payload, place.at, slot, 0).wait_recv()

    wait_handed(0, 0)
    each_away(wait_away)
    each_level(wait_handed)

    def take_ghosts(slot, carry):
        block = [landing[slot, row] for row in range(9)]
        fill_strengths(sides, GROUPS + slot, block[3:6], block[6:9])
        fill_places(sides, GROUPS + slot, block[0:3])
        return carry

    lax.fori_loop(0, 27, take_ghosts, 0)
    live = count_ref[0]
    near_pass(
        0, live, target_ref, from_ref, target_row[...], group_row[...], sides, targets, pairs, near
    )
    total = contrib[pl.ds(pl.multiple_of(gx * CELL_DEV, CELL_DEV), CELL_DEV), :]

    def wait_line(step, carry):
        line_copy(step).wait()
        return carry

    lax.fori_loop(1, nx, wait_line, 0)
    for step in range(1, nx):
        total = total + arrived[step]
    full = jnp.concatenate([total, jnp.zeros((TILE - CELL_DEV, 2 * TILE), F32)], axis=0)
    table_ref[pl.ds(0, TILE), :] = full[:, :TILE].T
    table_ref[pl.ds(TILE, TILE), :] = full[:, TILE:].T
    def far_pass(group):
        return far_force(
            [offset[group, row] for row in range(3)],
            [own[group, 3 + row] for row in range(3)],
            [own[group, 6 + row] for row in range(3)],
            cell_ref[pl.ds(8 * group, 8), :],
            table_ref,
        )

    for group in range(GROUPS):
        coupling = far_pass(group)
        for row in range(3):
            total = FAR_SCALE * coupling[row] + NEAR_SCALE * near[pl.ds(32 * row + 8 * group, 8), :]
            moved = offset[group, row] + STEP_SIZE * total
            force[group, row] = total
            offset[group, row] = moved
            own[group, row] = base[group, row] + moved
    for ghost in range(GHOST_DEV):
        tile = ghost_ref[ghost]
        for row in range(3):
            payload_next[row, pl.ds(ghost, 1), :] = own[tile // 8, row, pl.ds(lax.rem(tile, 8), 1), :]
    start_next, wait_next, wait_next_sent = exchange(
        place, lambda slot: payload_next, lambda slot: landing_next.at[slot], next_send, next_recv
    )
    each_slot(start_next)

    for group in range(GROUPS):
        coupling = far_pass(group)
        for row in range(3):
            far[group, row] = coupling[row]
        places = [own[group, row] for row in range(3)]
        fill_places(sides, group, places)
        fill_across_places(across, group, places)
    fill_targets(across, targets, False)
    low_ids = lax.broadcasted_iota(jnp.int32, (256, WIDTH), 0)

    def fill_lowers(block, carry):
        lanes = pl.ds(pl.multiple_of(block * WIDTH, WIDTH), WIDTH)
        for end in range(2):
            lower = dest_ref[pl.ds(end, 1), lanes] & 255
            lowers[block, :, pl.ds(end * WIDTH, WIDTH)] = jnp.where(
                low_ids == lower, 1.0, 0.0
            ).astype(BF16)
        return carry

    lax.fori_loop(0, SEG // WIDTH, fill_lowers, 0)

    def take_next(slot, carry):
        fill_places(sides, GROUPS + slot, [landing_next[slot, row] for row in range(3)])
        return carry

    each_slot(wait_next)
    lax.fori_loop(0, 27, take_next, 0)
    near_pass(
        1, live, target_ref, from_ref, target_row[...], group_row[...], sides, targets, pairs, near
    )
    for group in range(GROUPS):
        for row in range(3):
            total = FAR_SCALE * far[group, row] + NEAR_SCALE * near[pl.ds(32 * row + 8 * group, 8), :]
            moved = offset[group, row] + STEP_SIZE * total
            half = 0.5 * (force[group, row] + total)
            for tile in range(8):
                lanes = pl.ds((8 * group + tile) * TILE, TILE)
                moved_ref[pl.ds(row, 1), lanes] = moved[tile : tile + 1]
                values[pl.ds(row, 1), lanes] = half[tile : tile + 1]

    save_moved = pltpu.make_async_copy(moved_ref, moved_hbm, out_sem.at[0])
    save_moved.start()

    def scatter(first, count, totals):
        totals[...] = jnp.zeros(totals.shape, F32)
        high_ids = lax.broadcasted_iota(jnp.int32, (count, WIDTH), 0) + first

        def add(block, carry):
            lanes = pl.ds(pl.multiple_of(block * WIDTH, WIDTH), WIDTH)
            parts = [halves_of(values[pl.ds(row, 1), lanes]) for row in range(3)]
            lefts = []
            for end in range(2):
                dest = dest_ref[pl.ds(end, 1), lanes]
                slot = dest >> 12
                first_row = jnp.where(slot > 13, 12 + 4 * slot, 16 + 4 * slot)
                upper = jnp.where(slot == 13, 0, first_row) + ((dest & (SEG - 1)) >> 8)
                chosen = high_ids == upper
                lefts.append(
                    [
                        jnp.where(chosen, parts[row][piece], 0.0)
                        for row in range(3)
                        for piece in range(2)
                    ]
                )
            left = jnp.concatenate(
                [jnp.concatenate(both, axis=1) for both in zip(*lefts)], axis=0
            ).astype(BF16)
            totals[...] += lax.dot_general(left, lowers[block], NT, preferred_element_type=F32)
            return carry

        lax.fori_loop(0, SEG // WIDTH, add, 0)

    scatter(16, 104, sums)
    for row in range(3):
        for slot in range(27):
            if slot == 13:
                continue
            at = 208 * row + 4 * (slot - (slot > 13))
            both = sums[pl.ds(at, 4), :] + sums[pl.ds(at + 104, 4), :]
            leaving[slot, row, pl.ds(0, 4), :] = both[:, :TILE]
            leaving[slot, row, pl.ds(4, 4), :] = both[:, TILE:]
    start_node, wait_node, wait_node_sent = exchange(
        place, lambda slot: leaving.at[slot], lambda slot: landed.at[slot], node_send, node_recv
    )
    each_slot(start_node)
    scatter(0, 16, centre)
    middle = [
        centre[pl.ds(32 * row, 16), :] + centre[pl.ds(32 * row + 16, 16), :] for row in range(3)
    ]
    for row in range(3):
        for part in range(4, 16):
            nodes_ref[pl.ds(row, 1), pl.ds(256 * part, 256)] = middle[row][part : part + 1]
    inner = pl.ds(1024, SEG - 1024)
    save_inner = pltpu.make_async_copy(
        nodes_ref.at[:, inner], nodes_hbm.at[:, inner], out_sem.at[1]
    )
    save_inner.start()
    each_slot(wait_node)
    for row in range(3):
        total = landed[0, row]
        for slot in range(1, 27):
            if slot != 13:
                total = total + landed[slot, row]
        for part in range(4):
            for half in range(2):
                lanes = slice(TILE * half, TILE * half + TILE)
                nodes_ref[pl.ds(row, 1), pl.ds(256 * part + TILE * half, TILE)] = (
                    middle[row][part : part + 1, lanes]
                    + total[4 * half + part : 4 * half + part + 1]
                )

    outer = pl.ds(0, 1024)
    save_outer = pltpu.make_async_copy(
        nodes_ref.at[:, outer], nodes_hbm.at[:, outer], out_sem.at[2]
    )
    save_outer.start()

    each_level(lambda x, z: level_copy(x, z).wait_send())
    partner_copy().wait_send()
    each_away(lambda x, z: away_copy(x, z).wait_send())
    each_level(lambda x, z: handed_copy(x, z).wait_send())
    each_slot(wait_next_sent)
    each_slot(wait_node_sent)
    for save in (save_moved, save_inner, save_outer):
        save.wait()


def on_device(
    sizes,
    seg_rel,
    burgers,
    line_vec,
    seg_cell,
    ghost_tiles,
    ghost_count,
    pair_target,
    pair_source,
    pair_group,
    pair_count,
    node_dest,
):
    nx, ny, nz = sizes
    plane = ny * nz
    cell = seg_cell.reshape(SEG // TILE, TILE)
    shape = jax.ShapeDtypeStruct
    dma = pltpu.SemaphoreType.DMA
    block = (GROUPS, 3, 8, TILE)
    buffers = [
        (3, SEG),
        (3, SEG),
        (3, SEG),
        (3, SEG),
        (3, SEG),
        (SEG // TILE, TILE, jnp.int32),
        (2, SEG, jnp.int32),
        (1, PAIRS, jnp.int32),
        (1, PAIRS, jnp.int32),
        (GROUPS, 9, 8, TILE),
        block,
        block,
        block,
        block,
        (9, GHOST_DEV, TILE),
        (27, 9, GHOST_DEV, TILE),
        (3, GHOST_DEV, TILE),
        (27, 3, GHOST_DEV, TILE),
        (40 * 32, TILE),
        (COMP * 32, TILE),
        (plane * CELL_DEV, 2 * TILE),
        (nx * CELL_DEV, 2 * TILE),
        (nx, CELL_DEV, 2 * TILE),
        (2 * TILE, TILE),
        ((GROUPS + 27) * SIDE, TILE),
        (GROUPS * ACROSS, TILE),
        (SEG // TILE, 48, 4 * TILE, BF16),
        (3 * PAIRS, TILE),
        (3 * SEG // TILE, TILE),
        (8, SEG),
        (SEG // WIDTH, 256, 2 * WIDTH, BF16),
        (96, 256),
        (624, 256),
        (27, 3, 8, TILE),
        (27, 3, 8, TILE),
    ]
    scratch = []
    for sides in buffers:
        kind = F32
        if not isinstance(sides[-1], int):
            sides, kind = sides[:-1], sides[-1]
        scratch.append(pltpu.VMEM(sides, kind))
    return pl.pallas_call(
        functools.partial(step_kernel, sizes),
        out_shape=(shape((3, SEG), F32), shape((3, SEG), F32)),
        in_specs=[pl.BlockSpec(memory_space=pl.ANY)] * 12,
        out_specs=(pl.BlockSpec(memory_space=pl.ANY),) * 2,
        scratch_shapes=[
            pltpu.SMEM((count,), jnp.int32) for count in (GHOST_DEV, 1, 1, PAIRS, PAIRS)
        ]
        + scratch
        + [dma((12,)), dma((3,))]
        + [dma((27,))] * 6
        + [dma((plane,))] * 2
        + [dma((nx,))] * 2,
        compiler_params=pltpu.CompilerParams(
            collective_id=0, has_side_effects=True, vmem_limit_bytes=56 << 20
        ),
        name="step",
    )(
        ghost_tiles,
        ghost_count,
        pair_count,
        pair_target,
        pair_source,
        seg_rel,
        burgers,
        line_vec,
        cell,
        node_dest,
        pair_target.reshape(1, PAIRS),
        pair_group.reshape(1, PAIRS),
    )


def solution(mesh):
    sizes = tuple(mesh.shape[name] for name in ("gx", "gy", "gz"))
    whole = ("gx", "gy", "gz")
    return jax.shard_map(
        functools.partial(on_device, sizes),
        mesh=mesh,
        in_specs=(P(None, whole),) * 3 + (P(whole),) * 7 + (P(None, whole),),
        out_specs=(P(None, whole), P(None, whole)),
        check_vma=False,
    )
```
